256 devices in a mesh: seq: 64 (over y, x_lo, z), lvl: 4 (over x_hi, core).
Axes of the slice: x: 4 (x_hi: 2, x_lo: 2; x = x_hi * 2 + x_lo), y: 4, z: 8, core: 2. Of those that a mesh axis runs over, the one named last changes fastest.
Arguments:
- hidden: bfloat16 [8192, 4096], P('seq', 'lvl'), may hold values from -6 to 6
- code_ids: int32 [8192, 4], P('seq'), may hold values from 0 to 2047
- lengths: int32 [4], replicated, may hold values from 1 to 4096, 8192 in all
- weight_in: bfloat16 [4096, 1024], P('lvl'), may hold values from -0.09375 to 0.09375
- weight_query: bfloat16 [1024, 1024], P(None, 'lvl'), may hold values from -0.1875 to 0.1875
- weight_key: bfloat16 [1024, 1024], P(None, 'lvl'), may hold values from -0.1875 to 0.1875
- weight_value: bfloat16 [1024, 1024], P(None, 'lvl'), may hold values from -0.1875 to 0.1875
- weight_out: bfloat16 [1024, 1024], P('lvl'), may hold values from -0.1875 to 0.1875
- norm_gain: float32 [1024], replicated, may hold values from 0.1 to 1.9
- tables: bfloat16 [2048, 4, 1024], P('seq', None, 'lvl'), may hold values from -6 to 6
- upstream: bfloat16 [8192, 4, 1024], P(('seq', 'lvl')), may hold values from -6 to 6
Outputs:
- output: bfloat16 [8192, 4, 1024], P(('seq', 'lvl'))
- hidden_grad: bfloat16 [8192, 4096], P('seq', 'lvl')
- table_grad: float32 [2048, 4, 1024], P('seq', None, 'lvl')
The draws below stay inside these ranges and needn't reach their ends.
Inputs may be any that keep to these rules, and one draw needn't show every extreme that they name: Dialogue lengths in frames; they sum to 8192 and the longest has exactly 4096 frames.
All inputs are finite; a program needn't handle non-finite values.
Results may differ from the reference program's by a relative error of at most 0.02.
Values may be sent and summed in bfloat16 or wider, within the bound.
A program may use at most 128 MiB of HBM per device.

```python
import math
import jax
import jax.numpy as jnp
import numpy as np
from jax import lax

TWIDTH = 4096
DWIDTH = 1024
HEADS = 16
VOCAB = 2048
LEVELS = 4
DIALOGS = 4
FRAMES = 8192


def plant(array, rng, smallest, top_value):
    longest = array.shape.index(max(array.shape))
    spots = []
    for shift in (0, 1):
        where = [jax.random.randint(jax.random.fold_in(rng, axis), (), 0, length) for axis, length in enumerate(array.shape)]
        where[longest] = (where[longest] + shift) % array.shape[longest]
        spots.append(tuple(where))
    return array.at[spots[0]].set(smallest).at[spots[1]].set(top_value)


def shard_levels(own_key, dims, shards, low, top_value):
    level, own = 1.0, jax.random.fold_in(own_key, 6)
    for dim, blocks in shards:
        draws = jnp.exp(jax.random.uniform(jax.random.fold_in(own, dim), (blocks,), jnp.float32, low / len(shards), top_value / len(shards)))
        level = level * jnp.repeat(draws, dims[dim] // blocks).reshape([-1 if axis == dim else 1 for axis in range(len(dims))])
    return level


def rank_bounds(amount, lean):
    portions = [(1 << 20) // math.isqrt(grade ** lean) + 1 for grade in range(1, amount + 1)]
    deviation = 1 + sum(portions) // (1 << 30)
    return np.cumsum(np.array([max(1, weight // deviation) for weight in portions]))


def ranked(stream_key, extent, count, slope):
    table = rank_bounds(count, slope)
    ticket = jax.random.randint(jax.random.fold_in(stream_key, 1), extent, 0, int(table[count - 1]))
    rank = jnp.searchsorted(jnp.asarray(table, jnp.int32), ticket, side="right")
    return jax.random.permutation(jax.random.fold_in(stream_key, 2), count)[rank].astype(jnp.int32)


def profile(count, total, bound, skew):
    portions = [(1 << 20) // math.isqrt(rank ** skew) + 1 for rank in range(2, count + 1)]
    rest, holding = total - bound - (count - 1), [1] * (count - 1)
    while rest > 0:
        candidates = [i for i in range(count - 1) if holding[i] < bound]
        pool, budget = sum([portions[i] for i in candidates]), rest
        for i in candidates:
            addition = min(bound - holding[i], max(1, budget * portions[i] // pool), rest)
            holding[i] = holding[i] + addition
            rest = rest - addition
    return np.array([bound] + holding)


def ragged(stream_key, number_of, total, reach, slope):
    if number_of == 2:
        one = jax.random.randint(stream_key, (), max(1, total - reach), min(reach, total - 1) + 1)
        return jnp.stack([one, total - one])
    tallies = jnp.asarray(profile(number_of, total, reach, slope), jnp.int32)
    twos = (number_of - 1) // 2
    donor, sink = tallies[1:1 + 2 * twos:2], tallies[2:2 + 2 * twos:2]
    slack = jnp.minimum(donor - 1, reach - sink)
    shifted = jax.random.randint(jax.random.fold_in(stream_key, 1), (twos,), 0, 1 << 20) % (slack + 1)
    tallies = tallies.at[1:1 + 2 * twos:2].set(donor - shifted).at[2:2 + 2 * twos:2].set(sink + shifted)
    return tallies[jax.random.permutation(jax.random.fold_in(stream_key, 2), number_of)]


def gaussian(rng, extent, scale, limit, split=(), held_as=jnp.bfloat16):
    array = jax.random.normal(rng, extent, jnp.float32) * scale
    if len(split) > 0:
        array = shard_levels(rng, extent, split, -0.22, 0.18) * array
    return jnp.clip(array, min=-limit, max=limit).astype(held_as)


def setup_inputs(seed: int = 0) -> dict:
    seeds = jax.random.split(jax.random.key(seed), 12)
    hidden = gaussian(seeds[0], (FRAMES, TWIDTH), 1.0, 6.0, ((0, 64), (1, 4)))
    code_ids = plant(ranked(seeds[1], (FRAMES, LEVELS), VOCAB, 2), jax.random.fold_in(seeds[1], 3), 0, VOCAB - 1).astype(jnp.int32)
    lengths = ragged(seeds[2], DIALOGS, FRAMES, FRAMES // 2, 2).astype(jnp.int32)
    weight_in = gaussian(seeds[3], (TWIDTH, DWIDTH), TWIDTH ** -0.5, 0.09375, ((0, 4),))
    weight_query = gaussian(seeds[4], (DWIDTH, DWIDTH), DWIDTH ** -0.5, 0.1875, ((1, 4),))
    weight_key = gaussian(seeds[5], (DWIDTH, DWIDTH), DWIDTH ** -0.5, 0.1875, ((1, 4),))
    weight_value = gaussian(seeds[6], (DWIDTH, DWIDTH), DWIDTH ** -0.5, 0.1875, ((1, 4),))
    weight_out = gaussian(seeds[7], (DWIDTH, DWIDTH), DWIDTH ** -0.5, 0.1875, ((0, 4),))
    norm_gain = jnp.clip(1.0 + 0.18 * jax.random.normal(seeds[8], (DWIDTH,), jnp.float32), 0.1, 1.9)
    tables = gaussian(seeds[9], (VOCAB, LEVELS, DWIDTH), 1.0, 6.0, ((0, 64), (2, 4)))
    upstream = gaussian(seeds[10], (FRAMES, LEVELS, DWIDTH), 1.0, 6.0, ((0, 256),))
    return {"hidden": hidden, "code_ids": code_ids, "lengths": lengths, "weight_in": weight_in, "weight_query": weight_query, "weight_key": weight_key, "weight_value": weight_value, "weight_out": weight_out, "norm_gain": norm_gain, "tables": tables, "upstream": upstream}


EPSILON = 1e-05

def to_heads(tensor, head_size):
    return tensor.reshape(tensor.shape[0], tensor.shape[1], tensor.shape[2] // head_size, head_size)

def input_codes(code_ids, lengths):
    frames, levels = code_ids.shape
    earlier = jnp.concatenate([jnp.zeros((1,), jnp.int32), code_ids[:frames - 1, levels - 1]]).astype(jnp.int32)
    previous = jnp.concatenate([earlier[:, None], code_ids[:, :levels - 1]], axis=1).astype(jnp.int32)
    starts = (jnp.cumsum(lengths) - lengths).astype(jnp.int32)
    position = jnp.arange(frames, dtype=jnp.int32)
    begins = jnp.any(position[:, None] == starts[None, :], axis=1)
    first_level = jnp.where(begins, 0.0, 1.0).astype(jnp.float32)
    retain = jnp.concatenate([first_level[:, None], jnp.ones((frames, levels - 1), jnp.float32)], axis=1)
    return (previous, retain)

def project_flat(tensor, matrix):
    frames, levels, width = tensor.shape
    result = jnp.dot(tensor.reshape(frames * levels, width), matrix, preferred_element_type=jnp.float32)
    return result.reshape(frames, levels, -1)

def depth_block(stream, upstream, retain, norm_gain, weight_query, weight_key, weight_value, weight_out):
    frames, levels, width = stream.shape
    head_size = width // HEADS
    scaling = 1.0 / math.sqrt(head_size)
    scaler = lax.rsqrt(lax.optimization_barrier(jnp.mean(stream * stream, axis=-1, keepdims=True)) + EPSILON)
    unit_rows = stream * scaler
    normed = (unit_rows * norm_gain).astype(jnp.bfloat16)
    query_rows = project_flat(normed, weight_query).astype(jnp.bfloat16)
    key_rows = project_flat(normed, weight_key).astype(jnp.bfloat16)
    value_rows = project_flat(normed, weight_value).astype(jnp.bfloat16)
    query_heads = to_heads(query_rows, head_size).astype(jnp.float32)
    key_heads = to_heads(key_rows, head_size).astype(jnp.float32)
    value_heads = to_heads(value_rows, head_size).astype(jnp.float32)
    scores = jnp.einsum('flhs,fmhs->fhlm', query_heads, key_heads) * scaling
    causal = jnp.arange(levels)[None, :] <= jnp.arange(levels)[:, None]
    raised = jnp.where(causal, jnp.exp(scores), 0.0)
    weights = raised / lax.optimization_barrier(jnp.sum(raised, axis=-1, keepdims=True))
    weights_bf = weights.astype(jnp.bfloat16)
    mixture = jnp.einsum('fhlm,fmhs->flhs', weights_bf.astype(jnp.float32), value_heads)
    mixture = mixture.astype(jnp.bfloat16).reshape(frames, levels, width)
    output = (stream + project_flat(mixture, weight_out)).astype(jnp.bfloat16)
    grad_mixture = project_flat(upstream, weight_out.T).astype(jnp.bfloat16)
    grad_heads = to_heads(grad_mixture, head_size).astype(jnp.float32)
    grad_weights = jnp.einsum('flhs,fmhs->fhlm', grad_heads, value_heads)
    grad_value = jnp.einsum('fhlm,flhs->fmhs', weights_bf.astype(jnp.float32), grad_heads).astype(jnp.bfloat16)
    grad_scores = (weights * (grad_weights - lax.optimization_barrier(jnp.sum(weights * grad_weights, axis=-1, keepdims=True))) * scaling).astype(jnp.bfloat16)
    grad_query = jnp.einsum('fhlm,fmhs->flhs', grad_scores.astype(jnp.float32), key_heads).astype(jnp.bfloat16)
    grad_key = jnp.einsum('fhlm,flhs->fmhs', grad_scores.astype(jnp.float32), query_heads).astype(jnp.bfloat16)
    grad_normed = project_flat(grad_query.reshape(frames, levels, width), weight_query.T)
    grad_normed = grad_normed + project_flat(grad_key.reshape(frames, levels, width), weight_key.T)
    grad_normed = grad_normed + project_flat(grad_value.reshape(frames, levels, width), weight_value.T)
    grad_unit = norm_gain * grad_normed
    row_stat = lax.optimization_barrier(jnp.mean(unit_rows * grad_unit, axis=-1, keepdims=True))
    grad_stream = upstream.astype(jnp.float32) + scaler * (grad_unit - unit_rows * row_stat)
    embed_grad = (retain * grad_stream).astype(jnp.bfloat16)
    context_grad = lax.optimization_barrier(jnp.sum(grad_stream, axis=1)).astype(jnp.bfloat16)
    return (output, embed_grad, context_grad)

def reference(hidden, code_ids, lengths, weight_in, weight_query, weight_key, weight_value, weight_out, norm_gain, tables, upstream):
    previous, retain = input_codes(code_ids, lengths)
    context = jnp.dot(hidden, weight_in, preferred_element_type=jnp.float32)
    level_index = jnp.arange(LEVELS, dtype=jnp.int32)[None, :]
    embedded = tables[previous, level_index]
    stream = context[:, None, :] + retain[:, :, None] * embedded.astype(jnp.float32)
    block_rows = min(FRAMES, 512)
    count_blocks = FRAMES // block_rows

    def run_block(pieces):
        return depth_block(pieces[0], pieces[1], pieces[2][:, :, None], norm_gain, weight_query, weight_key, weight_value, weight_out)
    output, embed_grad, context_grad = lax.map(run_block, (stream.reshape(count_blocks, block_rows, LEVELS, DWIDTH), upstream.reshape(count_blocks, block_rows, LEVELS, DWIDTH), retain.reshape(count_blocks, block_rows, LEVELS)))
    output = output.reshape(FRAMES, LEVELS, DWIDTH)
    embed_grad = embed_grad.reshape(FRAMES * LEVELS, DWIDTH)
    context_grad = context_grad.reshape(FRAMES, DWIDTH)
    hidden_grad = jnp.dot(context_grad, weight_in.T, preferred_element_type=jnp.float32).astype(jnp.bfloat16)
    segment = (previous * LEVELS + level_index).reshape(-1).astype(jnp.int32)
    table_grad = jax.ops.segment_sum(embed_grad.astype(jnp.float32), segment, num_segments=VOCAB * LEVELS)
    table_grad = table_grad.reshape(VOCAB, LEVELS, DWIDTH)
    return (output, hidden_grad, table_grad)
```

```python
import math

import jax
import jax.numpy as jnp
from jax import lax
from jax.experimental import pallas as pl
from jax.experimental.pallas import tpu as pltpu
from jax.sharding import PartitionSpec as P

HEADS = 16
EPSILON = 1e-05
MESH = pl.DeviceIdType.MESH
F32 = jnp.float32
BF16 = jnp.bfloat16

NY, NZ = 4, 8
LV = 4
FR = 128
OWN = 32
COLS = 256
WIDTH = 1024
ENT = 32
RANGE = 512
PAIRS = [(a, b) for a in range(LV) for b in range(a + 1)]


def dot(a, b):
    return lax.dot_general(a, b, (((1,), (0,)), ((), ())), preferred_element_type=F32)


def dot_nt(a, b):
    return lax.dot_general(a, b, (((1,), (1,)), ((), ())), preferred_element_type=F32)


def kernel(
    codes_ref, lens_ref, gain_ref, tab_ref, up_ref, hid_ref, win_hbm, wq_hbm, wk_hbm, wv_hbm, wo_hbm,
    out_ref, hg_ref, tg_ref,
    win, wq, wk, wv, wo,
    nbr, prev, tab, oh, oht, ups, ctx_send, ctx_recv,
    look, relay, fin, stream_own, streams, normed, scale,
    qs, ks, vs, gms, prod, sums, mix, gqs, gks, gvs,
    pn, pn_own, pn_core, pn_mid, pn_x, stat_wide, stat, stat_col,
    opart, o_core, o_mid, o_x,
    eg, cgs, grads, zs_send, zs_recv, xs_send, xs_recv,
    local_sem, ssem, rsem,
):
    seq = lax.axis_index("seq")
    lvl = lax.axis_index("lvl")
    y = lax.div(seq, 16)
    xl = lax.rem(lax.div(seq, 8), 2)
    z = lax.rem(seq, 8)
    xh = lax.div(lvl, 2)
    core = lax.rem(lvl, 2)

    def device(dy=0, dx=0, dz=0, dh=0, dc=0):
        yy = lax.rem(y + dy + NY, NY)
        xx = 1 - xl if dx else xl
        zz = lax.rem(z + dz + NZ, NZ)
        hh = 1 - xh if dh else xh
        cc = 1 - core if dc else core
        return (yy * 16 + xx * 8 + zz, hh * 2 + cc)

    seq_next = (lax.rem(seq + 1, 64), lvl)
    seq_back = (lax.rem(seq + 63, 64), lvl)
    y_up, y_down, y_far = device(dy=1), device(dy=-1), device(dy=2)
    z_up, z_down = device(dz=1), device(dz=-1)
    x_near, x_far, mate, cross = device(dx=1), device(dh=1), device(dc=1), device(dh=1, dc=1)
    lvl_far = (1 - xh) * 2 + core
    lvl_mate = xh * 2 + 1 - core
    lvl_cross = (1 - xh) * 2 + 1 - core

    started = []

    def send(src, dst, target):
        i = len(started)
        copy = pltpu.make_async_remote_copy(
            src_ref=src, dst_ref=dst, send_sem=ssem.at[i], recv_sem=rsem.at[i],
            device_id=target, device_id_type=MESH,
        )
        copy.start()
        started.append(copy)
        return copy

    fetch = [
        pltpu.make_async_copy(a, b, local_sem.at[i])
        for i, (a, b) in enumerate(
            ((win_hbm, win), (wo_hbm, wo), (wq_hbm, wq), (wk_hbm, wk), (wv_hbm, wv))
        )
    ]
    for copy in fetch:
        copy.start()

    barrier = pltpu.get_barrier_semaphore()
    for source in (z_up, z_down, x_near, y_up, y_down, y_far, mate, x_far, cross, seq_back):
        pl.semaphore_signal(barrier, inc=1, device_id=source, device_id_type=MESH)

    def rows(start, size):
        return pl.ds(pl.multiple_of(start, size), size)

    def block_rows(xx, zz):
        return rows((xx * 8 + lax.rem(zz + NZ, NZ)) * ENT, ENT)

    own_rows = block_rows(xl, z)
    own_frames = rows(lvl * OWN, OWN)
    tab[:, own_rows, :] = tab_ref[...]
    ups[:, own_frames, :] = up_ref[...]

    pl.semaphore_wait(barrier, 10)

    code_copy = send(codes_ref, nbr, seq_next)
    x_copy = send(tab.at[:, own_rows], tab.at[:, own_rows], x_near)
    plus, minus = [], []
    plus.append([send(tab.at[:, own_rows], tab.at[:, own_rows], z_up)])
    minus.append([send(tab.at[:, own_rows], tab.at[:, own_rows], z_down)])
    up_far = send(ups.at[:, own_frames], ups.at[:, own_frames], x_far)
    up_mate = send(ups.at[:, own_frames], ups.at[:, own_frames], mate)

    fetch[0].wait()
    part = dot(hid_ref[...], win[...])
    for b in range(4):
        ctx_send[b] = part[:, b * COLS : (b + 1) * COLS].astype(BF16)
    ctx_copies = [
        send(ctx_send.at[lvl_far], ctx_recv.at[0], x_far),
        send(ctx_send.at[lvl_mate], ctx_recv.at[1], mate),
        send(ctx_send.at[lvl_cross], ctx_recv.at[2], cross),
    ]

    x_copy.wait_recv()
    near_rows = block_rows(1 - xl, z)
    plus[0].append(send(tab.at[:, near_rows], tab.at[:, near_rows], z_up))
    minus[0].append(send(tab.at[:, near_rows], tab.at[:, near_rows], z_down))

    code_copy.wait_recv()
    lane8 = lax.broadcasted_iota(jnp.int32, (8, FR), 1)
    sub8 = lax.broadcasted_iota(jnp.int32, (8, FR), 0)
    own_codes = codes_ref[...]
    shifted = pltpu.roll(own_codes, 1, 1)
    incoming = pltpu.roll(nbr[...], 1, 1)
    incoming = jnp.where(jnp.broadcast_to(seq, (8, FR)) == 0, 0, incoming)
    shifted = jnp.where(lane8 == 0, incoming, shifted)
    first_row = jnp.broadcast_to(shifted[LV - 1 : LV, :], (8, FR))
    prev[0] = jnp.where(sub8 == 0, first_row, pltpu.roll(own_codes, 1, 0))
    code_y = [
        send(prev.at[0], prev.at[1], y_up),
        send(prev.at[0], prev.at[2], y_down),
        send(prev.at[0], prev.at[3], y_far),
    ]

    def ring(t):
        last_plus, last_minus = plus[t - 1], minus[t - 1]
        new_plus, new_minus = [], []
        for j, xx in enumerate((xl, 1 - xl)):
            last_plus[j].wait_recv()
            block = block_rows(xx, z - t)
            new_plus.append(send(tab.at[:, block], tab.at[:, block], z_up))
            last_minus[j].wait_recv()
            if t < 3:
                block = block_rows(xx, z + t)
                new_minus.append(send(tab.at[:, block], tab.at[:, block], z_down))
        plus.append(new_plus)
        minus.append(new_minus)

    ring(1)
    up_far.wait_recv()
    far_frames = rows(lvl_far * OWN, OWN)
    up_pass = send(ups.at[:, far_frames], ups.at[:, far_frames], mate)

    for copy in code_y:
        copy.wait_recv()
    first = y * RANGE
    by_lane = lax.broadcasted_iota(jnp.int32, (FR, RANGE), 1) + first
    by_row = lax.broadcasted_iota(jnp.int32, (RANGE, FR), 0) + first
    for slot in range(NY):
        codes = prev[slot]
        turned = jnp.transpose(
            jnp.concatenate([codes.astype(F32), jnp.zeros((FR - 8, FR), F32)], axis=0)
        ).astype(jnp.int32)
        for k in range(LV):
            column = jnp.broadcast_to(turned[:, k : k + 1], (FR, RANGE))
            oh[k, slot * FR : (slot + 1) * FR, :] = jnp.where(column == by_lane, 1.0, 0.0).astype(BF16)

    ring(2)
    for slot in range(NY):
        codes = prev[slot]
        for k in range(LV):
            row = jnp.broadcast_to(codes[k : k + 1, :], (RANGE, FR))
            oht[k, :, slot * FR : (slot + 1) * FR] = jnp.where(row == by_row, 1.0, 0.0).astype(BF16)

    ring(3)
    up_mate.wait_recv()
    up_pass.wait_recv()
    fetch[1].wait()
    for k in range(LV):
        gms[k] = dot_nt(ups[k], wo[...]).astype(BF16)
    for copy in ctx_copies:
        copy.wait_recv()
    context = (
        ctx_send[lvl].astype(F32) + ctx_recv[0].astype(F32)
        + ctx_recv[1].astype(F32) + ctx_recv[2].astype(F32)
    )
    frame = lax.broadcasted_iota(jnp.int32, (FR, COLS), 0) + seq * FR
    begin = jnp.int32(0)
    retain = jnp.ones((FR, COLS), F32)
    for i in range(4):
        retain = jnp.where(frame == begin, 0.0, retain)
        begin = begin + lens_ref[i]

    for copy in plus[3]:
        copy.wait_recv()

    step_up, step_down, last_up, last_down = [], [], [], []
    for k in range(LV):
        found = dot(oh[k], tab[k]).astype(BF16)
        for slot in range(NY):
            look[slot, k] = found[slot * FR : (slot + 1) * FR, :]
        if k < 2:
            step_up.append(send(look.at[3, k], relay.at[0, k], y_up))
            last_down.append(send(look.at[1, k], fin.at[1, k], y_down))
            last_up.append(None)
        else:
            step_down.append(send(look.at[3, k], relay.at[1, k - 2], y_down))
            last_up.append(send(look.at[2, k], fin.at[0, k], y_up))
            last_down.append(None)
    for k in range(2):
        step_up[k].wait_recv()
        look[2, k] = look[2, k] + relay[0, k]
        last_up[k] = send(look.at[2, k], fin.at[0, k], y_up)
        step_down[k].wait_recv()
        look[1, k + 2] = look[1, k + 2] + relay[1, k]
        last_down[k + 2] = send(look.at[1, k + 2], fin.at[1, k + 2], y_down)

    far, near, passed = [], [], []
    for k in range(LV):
        last_up[k].wait_recv()
        last_down[k].wait_recv()
        embedded = look[0, k].astype(F32) + fin[0, k].astype(F32) + fin[1, k].astype(F32)
        if k == 0:
            embedded = retain * embedded
        own = context + embedded
        stream_own[k] = own
        streams[lvl, k] = own.astype(BF16)
        far.append(send(streams.at[lvl, k], streams.at[lvl, k], x_far))
        near.append(send(streams.at[lvl, k], streams.at[lvl, k], mate))
    for copy in fetch[2:]:
        copy.wait()
    for k in range(LV):
        far[k].wait_recv()
        passed.append(send(streams.at[lvl_far, k], streams.at[lvl_far, k], mate))
    for k in range(LV):
        near[k].wait_recv()
        passed[k].wait_recv()

    def norm_body(i, carry):
        k = lax.div(i, 4)
        r = rows(lax.rem(i, 4) * 32, 32)
        blocks = [streams[b, k, r, :].astype(F32) for b in range(4)]
        total = blocks[0] * blocks[0]
        for b in range(1, 4):
            total = total + blocks[b] * blocks[b]
        scaler = lax.rsqrt(jnp.sum(total, axis=1, keepdims=True) * (1.0 / WIDTH) + EPSILON)
        scale[k, r, :] = jnp.broadcast_to(scaler, (32, 128))
        for b in range(4):
            normed[k, r, b * COLS : (b + 1) * COLS] = (
                blocks[b] * scaler * gain_ref[:, b * COLS : (b + 1) * COLS]
            ).astype(BF16)
        return carry

    lax.fori_loop(0, 16, norm_body, 0)

    all_normed = normed[...].reshape(LV * FR, WIDTH)
    qs[...] = dot(all_normed, wq[...]).astype(BF16).reshape(LV, FR, COLS)
    ks[...] = dot(all_normed, wk[...]).astype(BF16).reshape(LV, FR, COLS)
    vs[...] = dot(all_normed, wv[...]).astype(BF16).reshape(LV, FR, COLS)

    def product_body(i, carry):
        r = rows(i * 16, 16)
        q = [qs[k, r, :].astype(F32) for k in range(LV)]
        kk = [ks[k, r, :].astype(F32) for k in range(LV)]
        for p, (a, b) in enumerate(PAIRS):
            prod[p, r, :] = (q[a] * kk[b]).astype(BF16)
        g = [gms[k, r, :].astype(F32) for k in range(LV)]
        v = [vs[k, r, :].astype(F32) for k in range(LV)]
        for p, (a, b) in enumerate(PAIRS):
            prod[len(PAIRS) + p, r, :] = (g[a] * v[b]).astype(BF16)
        return carry

    lax.fori_loop(0, 8, product_body, 0)
    head_row = lax.shift_right_logical(lax.broadcasted_iota(jnp.int32, (COLS, COLS), 0), 6)
    head_col = lax.shift_right_logical(lax.broadcasted_iota(jnp.int32, (COLS, COLS), 1), 6)
    same_head = jnp.where(head_row == head_col, 1.0, 0.0).astype(BF16)

    def sum_body(p, carry):
        sums[p] = dot(prod[p], same_head)
        return carry

    lax.fori_loop(0, 2 * len(PAIRS), sum_body, 0)
    scaling = 1.0 / math.sqrt(WIDTH // HEADS)

    def attend_body(i, carry):
        r = rows(lax.div(i, 2) * 16, 16)
        c = rows(lax.rem(i, 2) * 128, 128)
        q = [qs[k, r, c].astype(F32) for k in range(LV)]
        kk = [ks[k, r, c].astype(F32) for k in range(LV)]
        v = [vs[k, r, c].astype(F32) for k in range(LV)]
        g = [gms[k, r, c].astype(F32) for k in range(LV)]
        grad_key = [None] * LV
        grad_value = [None] * LV
        p = 0
        for a in range(LV):
            raised = [jnp.exp(sums[p + b, r, c] * scaling) for b in range(a + 1)]
            total = raised[0]
            for b in range(1, a + 1):
                total = total + raised[b]
            inverse = 1.0 / total
            weights = [x * inverse for x in raised]
            rounded = [x.astype(BF16).astype(F32) for x in weights]
            slopes = [sums[len(PAIRS) + p + b, r, c] for b in range(a + 1)]
            mixed = rounded[0] * v[0]
            mean = weights[0] * slopes[0]
            for b in range(1, a + 1):
                mixed = mixed + rounded[b] * v[b]
                mean = mean + weights[b] * slopes[b]
            mix[a, r, c] = mixed.astype(BF16)
            grad_query = None
            for b in range(a + 1):
                grad_score = (weights[b] * (slopes[b] - mean) * scaling).astype(BF16).astype(F32)
                term_q = grad_score * kk[b]
                term_k = grad_score * q[a]
                term_v = rounded[b] * g[a]
                grad_query = term_q if b == 0 else grad_query + term_q
                grad_key[b] = term_k if a == b else grad_key[b] + term_k
                grad_value[b] = term_v if a == b else grad_value[b] + term_v
            gqs[a, r, c] = grad_query.astype(BF16)
            p += a + 1
        for b in range(LV):
            gks[b, r, c] = grad_key[b].astype(BF16)
            gvs[b, r, c] = grad_value[b].astype(BF16)
        return carry

    lax.fori_loop(0, 16, attend_body, 0)

    gq = gqs[...].reshape(LV * FR, COLS)
    gk = gks[...].reshape(LV * FR, COLS)
    gv = gvs[...].reshape(LV * FR, COLS)
    pn_copies = []
    for j, owner in enumerate((lvl_cross, lvl_mate, lvl_far, lvl)):
        w = rows(owner * COLS, COLS)
        partial = dot_nt(gq, wq[w, :]) + dot_nt(gk, wk[w, :]) + dot_nt(gv, wv[w, :])
        c = rows(owner * COLS, COLS)
        share = jnp.sum(normed[:, :, c].astype(F32).reshape(LV * FR, COLS) * partial, axis=1, keepdims=True)
        share = jnp.broadcast_to(share, (LV * FR, 128)).reshape(LV, FR, 128)
        stat_wide[...] = share if j == 0 else stat_wide[...] + share
        if j < 3:
            pn[j] = partial.astype(BF16).reshape(LV, FR, COLS)
        else:
            pn_own[...] = partial.reshape(LV, FR, COLS)
        if j < 2:
            pn_copies.append([send(pn.at[j, k], pn_core.at[j, k], mate) for k in range(LV)])
    pn_far = []
    for k in range(LV):
        pn_copies[0][k].wait_recv()
        pn_mid[k] = (pn[2, k].astype(F32) + pn_core[0, k].astype(F32)).astype(BF16)
        pn_far.append(send(pn_mid.at[k], pn_x.at[k], x_far))

    eye = lax.broadcasted_iota(jnp.int32, (FR, FR), 0) == lax.broadcasted_iota(jnp.int32, (FR, FR), 1)
    for k in range(LV):
        stat[0, k : k + 1, :] = jnp.sum(jnp.where(eye, stat_wide[k], 0.0), axis=0, keepdims=True)
    stat[0, LV:, :] = jnp.zeros((8 - LV, FR), F32)
    stat_copies = [
        send(stat.at[0], stat.at[1], x_far),
        send(stat.at[0], stat.at[2], mate),
        send(stat.at[0], stat.at[3], cross),
    ]

    opart[...] = dot(mix[...].reshape(LV * FR, COLS), wo[...]).astype(BF16).reshape(LV, FR, WIDTH)
    cross_frames = rows(lvl_cross * OWN, OWN)
    mate_frames = rows(lvl_mate * OWN, OWN)
    o_copies = [
        send(opart.at[:, cross_frames], o_core.at[0], mate),
        send(opart.at[:, mate_frames], o_core.at[1], mate),
    ]

    for copy in stat_copies:
        copy.wait_recv()
    stat_all = (stat[0] + stat[1] + stat[2] + stat[3]) * (1.0 / WIDTH)
    for k in range(LV):
        column = jnp.sum(
            jnp.where(eye, jnp.broadcast_to(stat_all[k : k + 1, :], (FR, FR)), 0.0), axis=1, keepdims=True
        )
        stat_col[k] = jnp.broadcast_to(column, (FR, 128))

    own_cols = rows(lvl * COLS, COLS)
    gain = gain_ref[:, own_cols]
    context_grad = None
    g_up, g_down = [], []
    for k in range(LV):
        pn_copies[1][k].wait_recv()
        pn_far[k].wait_recv()
        grad_normed = pn_own[k] + pn_core[1, k].astype(F32) + pn_x[k].astype(F32)
        scaler = scale[k][:, 0:1]
        unit = stream_own[k] * scaler
        grad = ups[k, :, own_cols].astype(F32) + scaler * (gain * grad_normed - unit * stat_col[k][:, 0:1])
        context_grad = grad if k == 0 else context_grad + grad
        eg[k, 0:FR, :] = (retain * grad if k == 0 else grad).astype(BF16)
        g_up.append(send(eg.at[k, 0:FR], eg.at[k, FR : 2 * FR], y_up))
        g_down.append(send(eg.at[k, 0:FR], eg.at[k, 2 * FR : 3 * FR], y_down))
    cgs[lvl] = context_grad.astype(BF16)
    cg_copies = [
        send(cgs.at[lvl], cgs.at[lvl], x_far),
        send(cgs.at[lvl], cgs.at[lvl], mate),
        send(cgs.at[lvl], cgs.at[lvl], cross),
    ]

    o_copies[0].wait_recv()
    o_mid[...] = (opart[:, far_frames, :].astype(F32) + o_core[0].astype(F32)).astype(BF16)
    o_far = send(o_mid, o_x, x_far)

    g_pass = []
    for k in range(2):
        g_up[k].wait_recv()
        g_pass.append(send(eg.at[k, FR : 2 * FR], eg.at[k, 3 * FR : 4 * FR], y_up))
    for k in range(2, 4):
        g_down[k].wait_recv()
        g_pass.append(send(eg.at[k, 2 * FR : 3 * FR], eg.at[k, 3 * FR : 4 * FR], y_down))

    for copy in cg_copies:
        copy.wait_recv()
    whole = jnp.concatenate([cgs[b] for b in range(4)], axis=1)
    hg_ref[...] = dot_nt(whole, win[...]).astype(BF16)

    def packed(xx, zz, k):
        return grads[k, block_rows(xx, zz), :]

    up_steps = [[], [], [], []]
    down_steps = [[], [], []]
    for t in range(4):
        for k in range(LV):
            if t == 0:
                if k < 2:
                    g_down[k].wait_recv()
                else:
                    g_up[k].wait_recv()
                g_pass[k].wait_recv()
                grads[k] = dot(oht[k], eg[k])
            if t > 0:
                up_steps[t - 1][k].wait_recv()
            for j in range(2):
                value = packed(xl if j == 0 else 1 - xl, z + 4 - t, k)
                if t > 0:
                    value = value + zs_recv[0, t - 1, k, j].astype(F32)
                zs_send[0, t, k, j] = value.astype(BF16)
            up_steps[t].append(send(zs_send.at[0, t, k], zs_recv.at[0, t, k], z_up))
            if t < 3:
                if t > 0:
                    down_steps[t - 1][k].wait_recv()
                for j in range(2):
                    value = packed(xl if j == 0 else 1 - xl, z - 3 + t, k)
                    if t > 0:
                        value = value + zs_recv[1, t - 1, k, j].astype(F32)
                    zs_send[1, t, k, j] = value.astype(BF16)
                down_steps[t].append(send(zs_send.at[1, t, k], zs_recv.at[1, t, k], z_down))

    o_copies[1].wait_recv()
    o_far.wait_recv()
    for k in range(LV):
        base = jnp.concatenate([streams[b, k, own_frames, :] for b in range(4)], axis=1).astype(F32)
        out_ref[k] = (
            base + opart[k, own_frames, :].astype(F32) + o_core[1, k].astype(F32) + o_x[k].astype(F32)
        ).astype(BF16)

    last = []
    for k in range(LV):
        up_steps[3][k].wait_recv()
        down_steps[2][k].wait_recv()
        value = (
            packed(1 - xl, z, k) + zs_recv[0, 3, k, 1].astype(F32) + zs_recv[1, 2, k, 1].astype(F32)
        )
        xs_send[k] = value.astype(BF16)
        last.append(send(xs_send.at[k], xs_recv.at[k], x_near))
    for k in range(LV):
        value = (
            packed(xl, z, k) + zs_recv[0, 3, k, 0].astype(F32) + zs_recv[1, 2, k, 0].astype(F32)
        )
        last[k].wait_recv()
        tg_ref[k] = value + xs_recv[k].astype(F32)

    for copy in started:
        copy.wait_send()


def shards(
    hidden, code_ids, lengths, weight_in, weight_query, weight_key, weight_value, weight_out,
    norm_gain, tables, upstream,
):
    codes = jnp.pad(code_ids.T, ((0, 8 - LV), (0, 0)))
    vmem = pl.BlockSpec(memory_space=pltpu.VMEM)
    hbm = pl.BlockSpec(memory_space=pl.ANY)
    smem = pl.BlockSpec(memory_space=pltpu.SMEM)

    def scratch(dtype, *shape):
        return pltpu.VMEM(shape, dtype)

    pairs = len(PAIRS)
    block = (LV, FR, COLS)
    out, hidden_grad, table_grad = pl.pallas_call(
        kernel,
        out_shape=(
            jax.ShapeDtypeStruct((LV, OWN, WIDTH), BF16),
            jax.ShapeDtypeStruct((FR, WIDTH), BF16),
            jax.ShapeDtypeStruct((LV, ENT, COLS), F32),
        ),
        in_specs=[vmem, smem, vmem, vmem, vmem, vmem, hbm, hbm, hbm, hbm, hbm],
        out_specs=(vmem, vmem, vmem),
        scratch_shapes=[
            scratch(BF16, WIDTH, WIDTH),
            scratch(BF16, WIDTH, COLS),
            scratch(BF16, WIDTH, COLS),
            scratch(BF16, WIDTH, COLS),
            scratch(BF16, COLS, WIDTH),
            scratch(jnp.int32, 8, FR),
            scratch(jnp.int32, NY, 8, FR),
            scratch(BF16, LV, RANGE, COLS),
            scratch(BF16, LV, NY * FR, RANGE),
            scratch(BF16, LV, RANGE, NY * FR),
            scratch(BF16, LV, FR, WIDTH),
            scratch(BF16, 4, FR, COLS),
            scratch(BF16, 3, FR, COLS),
            scratch(BF16, NY, *block),
            scratch(BF16, 2, 2, FR, COLS),
            scratch(BF16, 2, *block),
            scratch(F32, *block),
            scratch(BF16, 4, *block),
            scratch(BF16, LV, FR, WIDTH),
            scratch(F32, LV, FR, 128),
            scratch(BF16, *block),
            scratch(BF16, *block),
            scratch(BF16, *block),
            scratch(BF16, *block),
            scratch(BF16, 2 * pairs, FR, COLS),
            scratch(F32, 2 * pairs, FR, COLS),
            scratch(BF16, *block),
            scratch(BF16, *block),
            scratch(BF16, *block),
            scratch(BF16, *block),
            scratch(BF16, 3, *block),
            scratch(F32, *block),
            scratch(BF16, 2, *block),
            scratch(BF16, *block),
            scratch(BF16, *block),
            scratch(F32, LV, FR, 128),
            scratch(F32, 4, 8, FR),
            scratch(F32, LV, FR, 128),
            scratch(BF16, LV, FR, WIDTH),
            scratch(BF16, 2, LV, OWN, WIDTH),
            scratch(BF16, LV, OWN, WIDTH),
            scratch(BF16, LV, OWN, WIDTH),
            scratch(BF16, LV, NY * FR, COLS),
            scratch(BF16, 4, FR, COLS),
            scratch(F32, LV, RANGE, COLS),
            scratch(BF16, 2, 4, LV, 2, ENT, COLS),
            scratch(BF16, 2, 4, LV, 2, ENT, COLS),
            scratch(BF16, LV, ENT, COLS),
            scratch(BF16, LV, ENT, COLS),
            pltpu.SemaphoreType.DMA((5,)),
            pltpu.SemaphoreType.DMA((128,)),
            pltpu.SemaphoreType.DMA((128,)),
        ],
        compiler_params=pltpu.CompilerParams(
            collective_id=0, has_side_effects=True, vmem_limit_bytes=50 << 20
        ),
        name="layer",
    )(
        codes,
        lengths,
        norm_gain.reshape(1, WIDTH),
        jnp.transpose(tables, (1, 0, 2)),
        jnp.transpose(upstream, (1, 0, 2)),
        hidden,
        weight_in,
        weight_query,
        weight_key,
        weight_value,
        weight_out,
    )
    return (
        jnp.transpose(out, (1, 0, 2)),
        hidden_grad,
        jnp.transpose(table_grad, (1, 0, 2)),
    )


def solution(mesh):
    placed = (
        P("seq", "lvl"),
        P("seq", None),
        P(),
        P("lvl", None),
        P(None, "lvl"),
        P(None, "lvl"),
        P(None, "lvl"),
        P("lvl", None),
        P(),
        P("seq", None, "lvl"),
        P(("seq", "lvl"), None, None),
    )
    return jax.shard_map(
        shards,
        mesh=mesh,
        in_specs=placed,
        out_specs=(P(("seq", "lvl"), None, None), P("seq", "lvl"), P("seq", None, "lvl")),
        check_vma=False,
    )
```

```python
import math

import jax
import jax.numpy as jnp
from jax import lax
from jax.experimental import pallas as pl
from jax.experimental.pallas import tpu as pltpu
from jax.sharding import PartitionSpec as P

HEADS = 16
EPSILON = 1e-05
MESH = pl.DeviceIdType.MESH
F32 = jnp.float32
BF16 = jnp.bfloat16

NY, NZ = 4, 8
LV = 4
FR = 128
OWN = 32
COLS = 256
WIDTH = 1024
ENT = 32
RANGE = 512
COPIES = 192


def dot(a, b):
    return lax.dot_general(a, b, (((1,), (0,)), ((), ())), preferred_element_type=F32)


def dot_nt(a, b):
    return lax.dot_general(a, b, (((1,), (1,)), ((), ())), preferred_element_type=F32)


def kernel(
    codes_hbm, lens_hbm, gain_hbm, tab_hbm, up_hbm, hid_hbm, win_hbm, wq_hbm, wk_hbm, wv_hbm, wo_hbm,
    out_ref, hg_ref, tg_ref,
    codes_ref, lens_ref, gain_ref, hid_ref, win, wq, wk, wv, wo,
    nbr, prev, tab, oh, oht, ups, ctx_send, ctx_core, ctx_mid, ctx_x,
    look, relay, fin, stream_own, streams, normed, scale,
    qs, ks, vs, gms, prod, sums, mix, gqs, gks, gvs, gk_sum, gv_sum,
    pn, pn_own, pn_core, pn_mid, pn_x, stat_wide, stat, stat_col,
    opart, o_core, o_mid, o_x,
    eg, cgs, grads, f3_send, f3_recv, f4_send, f4_recv, c1_send, c1_recv, c2_send, c2_recv, d_send, d_recv,
    local_sem, ssem, rsem,
):
    seq = lax.axis_index("seq")
    lvl = lax.axis_index("lvl")
    y = lax.div(seq, 16)
    xl = lax.rem(lax.div(seq, 8), 2)
    z = lax.rem(seq, 8)
    xh = lax.div(lvl, 2)
    core = lax.rem(lvl, 2)

    def device(dy=0, dx=0, dz=0, dh=0, dc=0):
        yy = lax.rem(y + dy + NY, NY)
        xx = 1 - xl if dx else xl
        zz = lax.rem(z + dz + NZ, NZ)
        hh = 1 - xh if dh else xh
        cc = 1 - core if dc else core
        return (yy * 16 + xx * 8 + zz, hh * 2 + cc)

    seq_next = (lax.rem(seq + 1, 64), lvl)
    seq_back = (lax.rem(seq + 63, 64), lvl)
    y_up, y_down, y_far = device(dy=1), device(dy=-1), device(dy=2)
    z_up, z_down, z_up2, z_down2 = device(dz=1), device(dz=-1), device(dz=2), device(dz=-2)
    x_near, x_far, mate, cross = device(dx=1), device(dh=1), device(dc=1), device(dh=1, dc=1)
    lvl_far = (1 - xh) * 2 + core
    lvl_mate = xh * 2 + 1 - core
    lvl_cross = (1 - xh) * 2 + 1 - core

    started = []

    def send(src, dst, target):
        i = len(started)
        copy = pltpu.make_async_remote_copy(
            src_ref=src, dst_ref=dst, send_sem=ssem.at[i], recv_sem=rsem.at[i],
            device_id=target, device_id_type=MESH,
        )
        copy.start()
        started.append(copy)
        return copy

    def push(ref, target):
        return send(ref, ref, target)

    def rows(start, size):
        return pl.ds(pl.multiple_of(start, size), size)

    def block_rows(xx, zz):
        return rows((xx * 8 + lax.rem(zz + NZ, NZ)) * ENT, ENT)

    own_rows = block_rows(xl, z)
    own_frames = rows(lvl * OWN, OWN)
    far_frames = rows(lvl_far * OWN, OWN)
    mate_frames = rows(lvl_mate * OWN, OWN)
    cross_frames = rows(lvl_cross * OWN, OWN)

    codes_ref[...] = jnp.zeros((8, FR), jnp.int32)
    fetch = {}
    for i, (name, a, b) in enumerate(
        (
            ("tab", tab_hbm, tab.at[:, own_rows]),
            ("codes", codes_hbm, codes_ref.at[0:LV]),
            ("hid", hid_hbm, hid_ref),
            ("win", win_hbm, win),
            ("ups", up_hbm, ups.at[:, own_frames]),
            ("lens", lens_hbm, lens_ref),
            ("gain", gain_hbm, gain_ref),
            ("wo", wo_hbm, wo),
            ("wq", wq_hbm, wq),
            ("wk", wk_hbm, wk),
            ("wv", wv_hbm, wv),
        )
    ):
        fetch[name] = pltpu.make_async_copy(a, b, local_sem.at[i])
        fetch[name].start()

    barrier = pltpu.get_barrier_semaphore()
    for source in (z_up, z_down, z_up2, z_down2, x_near, y_up, y_down, y_far, mate, x_far, cross, seq_back):
        pl.semaphore_signal(barrier, inc=1, device_id=source, device_id_type=MESH)
    fetch["hid"].wait()
    fetch["win"].wait()
    part = dot(hid_ref[...], win[...])
    for b in range(4):
        ctx_send[b] = part[:, b * COLS : (b + 1) * COLS].astype(BF16)
    fetch["tab"].wait()
    fetch["codes"].wait()
    pl.semaphore_wait(barrier, 12)

    def block(half, xx, zz):
        return tab.at[2 * half : 2 * half + 2, block_rows(xx, zz)]

    own = [block(h, xl, z) for h in range(2)]
    up2, down2, up1, down1, near_own = [], [], [], [], []
    for h in range(2):
        up2.append(push(own[h], z_up2))
        down2.append(push(own[h], z_down2))
        near_own.append(push(own[h], x_near))
        up1.append(push(own[h], z_up))
        down1.append(push(own[h], z_down))
    code_copy = send(codes_ref, nbr, seq_next)
    ctx_copies = [
        send(ctx_send.at[lvl_cross], ctx_core.at[0], mate),
        send(ctx_send.at[lvl_mate], ctx_core.at[1], mate),
    ]
    fetch["ups"].wait()
    up_mate = [push(ups.at[k, own_frames], mate) for k in range(LV)]

    near2, up3, down3, near1 = [], [], [], []
    for h in range(2):
        up2[h].wait_recv()
        near2.append(push(block(h, xl, z - 2), x_near))
        up3.append(push(block(h, xl, z - 2), z_up))
        if h == 0:
            end_up = push(block(0, xl, z - 2), z_up2)
        down2[h].wait_recv()
        near2.append(push(block(h, xl, z + 2), x_near))
        down3.append(push(block(h, xl, z + 2), z_down))
        if h == 1:
            end_down = push(block(1, xl, z + 2), z_down2)
    for h in range(2):
        up1[h].wait_recv()
        near1.append(push(block(h, xl, z - 1), x_near))
        down1[h].wait_recv()
        near1.append(push(block(h, xl, z + 1), x_near))

    code_copy.wait_recv()
    lane8 = lax.broadcasted_iota(jnp.int32, (8, FR), 1)
    sub8 = lax.broadcasted_iota(jnp.int32, (8, FR), 0)
    own_codes = codes_ref[...]
    shifted = pltpu.roll(own_codes, 1, 1)
    incoming = pltpu.roll(nbr[...], 1, 1)
    incoming = jnp.where(jnp.broadcast_to(seq, (8, FR)) == 0, 0, incoming)
    shifted = jnp.where(lane8 == 0, incoming, shifted)
    first_row = jnp.broadcast_to(shifted[LV - 1 : LV, :], (8, FR))
    prev[0] = jnp.where(sub8 == 0, first_row, pltpu.roll(own_codes, 1, 0))
    code_y = [
        send(prev.at[0], prev.at[1], y_up),
        send(prev.at[0], prev.at[2], y_down),
        send(prev.at[0], prev.at[3], y_far),
    ]
    ctx_copies[0].wait_recv()
    ctx_mid[...] = (ctx_send[lvl_far].astype(F32) + ctx_core[0].astype(F32)).astype(BF16)
    ctx_far = send(ctx_mid, ctx_x, x_far)

    for copy in code_y:
        copy.wait_recv()
    first = y * RANGE
    by_lane = lax.broadcasted_iota(jnp.int32, (FR, RANGE), 1) + first
    by_row = lax.broadcasted_iota(jnp.int32, (RANGE, FR), 0) + first
    for slot in range(NY):
        codes = prev[slot]
        turned = jnp.transpose(
            jnp.concatenate([codes.astype(F32), jnp.zeros((FR - 8, FR), F32)], axis=0)
        ).astype(jnp.int32)
        for k in range(LV):
            column = jnp.broadcast_to(turned[:, k : k + 1], (FR, RANGE))
            oh[k, slot * FR : (slot + 1) * FR, :] = jnp.where(column == by_lane, 1.0, 0.0).astype(BF16)

    far_up, far_down = [], []
    for h in range(2):
        near2[2 * h].wait_recv()
        far_up.append(push(block(h, 1 - xl, z - 2), z_up))
        if h == 0:
            far_end_up = push(block(0, 1 - xl, z - 2), z_up2)
        near2[2 * h + 1].wait_recv()
        far_down.append(push(block(h, 1 - xl, z + 2), z_down))
        if h == 1:
            far_end_down = push(block(1, 1 - xl, z + 2), z_down2)
    up_far = [push(ups.at[k, own_frames], x_far) for k in range(LV)]

    for slot in range(NY):
        codes = prev[slot]
        for k in range(LV):
            row = jnp.broadcast_to(codes[k : k + 1, :], (RANGE, FR))
            oht[k, :, slot * FR : (slot + 1) * FR] = jnp.where(row == by_row, 1.0, 0.0).astype(BF16)
    fetch["lens"].wait()
    frame = lax.broadcasted_iota(jnp.int32, (FR, COLS), 0) + seq * FR
    begin = jnp.int32(0)
    retain = jnp.ones((FR, COLS), F32)
    for i in range(4):
        retain = jnp.where(frame == begin, 0.0, retain)
        begin = begin + lens_ref[i]
    ctx_copies[1].wait_recv()
    ctx_far.wait_recv()
    context = ctx_send[lvl].astype(F32) + ctx_core[1].astype(F32) + ctx_x[...].astype(F32)

    top, low = slice(0, FR // 2), slice(FR // 2, FR)
    relay_up, relay_down = [], []
    fin_up = [[None, None] for _ in range(LV)]
    fin_down = [[None, None] for _ in range(LV)]

    def find(k):
        found = dot(oh[k], tab[k]).astype(BF16)
        for slot in (3, 2, 1, 0):
            look[slot, k] = found[slot * FR : (slot + 1) * FR, :]
        relay_up.append(send(look.at[3, k, top], relay.at[0, k], y_up))
        relay_down.append(send(look.at[3, k, low], relay.at[1, k], y_down))

    def direct(k):
        fin_up[k][1] = send(look.at[2, k, low], fin.at[0, k, low], y_up)
        fin_down[k][0] = send(look.at[1, k, top], fin.at[1, k, top], y_down)

    def relayed(k):
        relay_up[k].wait_recv()
        look[2, k, top] = look[2, k, top] + relay[0, k]
        fin_up[k][0] = send(look.at[2, k, top], fin.at[0, k, top], y_up)
        relay_down[k].wait_recv()
        look[1, k, low] = look[1, k, low] + relay[1, k]
        fin_down[k][1] = send(look.at[1, k, low], fin.at[1, k, low], y_down)

    far, near, passed = [], [], []

    def stream(k):
        for copy in fin_up[k] + fin_down[k]:
            copy.wait_recv()
        embedded = look[0, k].astype(F32) + fin[0, k].astype(F32) + fin[1, k].astype(F32)
        if k == 0:
            embedded = retain * embedded
        own = context + embedded
        stream_own[k] = own
        streams[lvl, k] = own.astype(BF16)
        far.append(push(streams.at[lvl, k], x_far))
        near.append(push(streams.at[lvl, k], mate))

    def pass_stream(k):
        far[k].wait_recv()
        passed.append(push(streams.at[lvl_far, k], mate))

    def blocks_in(h):
        for copy in (up3[h], down3[h], near_own[h], near1[2 * h], near1[2 * h + 1], far_up[h], far_down[h]):
            copy.wait_recv()

    blocks_in(0)
    end_up.wait_recv()
    far_end_up.wait_recv()
    find(0)
    find(1)
    direct(0)
    blocks_in(1)
    end_down.wait_recv()
    far_end_down.wait_recv()
    find(2)
    find(3)
    direct(1)
    relayed(0)
    relayed(1)
    direct(2)
    relayed(2)
    direct(3)
    relayed(3)
    stream(0)
    stream(1)
    stream(2)
    stream(3)
    up_pass = []
    for k in range(LV):
        up_far[k].wait_recv()
        up_pass.append(push(ups.at[k, far_frames], mate))
    pass_stream(0)
    pass_stream(1)
    fetch["wo"].wait()
    for k in range(LV):
        up_mate[k].wait_recv()
        up_pass[k].wait_recv()
    gms[...] = dot_nt(ups[...].reshape(LV * FR, WIDTH), wo[...]).astype(BF16).reshape(LV, FR, COLS)
    for name in ("gain", "wq", "wk", "wv"):
        fetch[name].wait()

    head_row = lax.shift_right_logical(lax.broadcasted_iota(jnp.int32, (COLS, COLS), 0), 6)
    head_col = lax.shift_right_logical(lax.broadcasted_iota(jnp.int32, (COLS, COLS), 1), 6)
    same_head = jnp.where(head_row == head_col, 1.0, 0.0).astype(BF16)
    scaling = 1.0 / math.sqrt(WIDTH // HEADS)

    def norm(a):
        near[a].wait_recv()
        passed[a].wait_recv()

        def norm_body(i, carry):
            r = rows(i * 32, 32)
            blocks = [streams[b, a, r, :].astype(F32) for b in range(4)]
            total = blocks[0] * blocks[0]
            for b in range(1, 4):
                total = total + blocks[b] * blocks[b]
            scaler = lax.rsqrt(jnp.sum(total, axis=1, keepdims=True) * (1.0 / WIDTH) + EPSILON)
            scale[a, r, :] = jnp.broadcast_to(scaler, (32, 128))
            for b in range(4):
                normed[a, r, b * COLS : (b + 1) * COLS] = (
                    blocks[b] * scaler * gain_ref[:, b * COLS : (b + 1) * COLS]
                ).astype(BF16)
            return carry

        lax.fori_loop(0, 4, norm_body, 0)

    def attend_level(a, base):
        def attend_body(i, carry):
            r = rows(lax.div(i, 2) * 16, 16)
            c = rows(lax.rem(i, 2) * 128, 128)
            q = qs[a, r, c].astype(F32)
            g = gms[a, r, c].astype(F32)
            raised = [jnp.exp(sums[base + b, r, c] * scaling) for b in range(a + 1)]
            total = raised[0]
            for b in range(1, a + 1):
                total = total + raised[b]
            inverse = 1.0 / total
            weights = [x * inverse for x in raised]
            rounded = [x.astype(BF16).astype(F32) for x in weights]
            slopes = [sums[base + a + 1 + b, r, c] for b in range(a + 1)]
            mixed = rounded[0] * vs[0, r, c].astype(F32)
            mean = weights[0] * slopes[0]
            for b in range(1, a + 1):
                mixed = mixed + rounded[b] * vs[b, r, c].astype(F32)
                mean = mean + weights[b] * slopes[b]
            mix[a, r, c] = mixed.astype(BF16)
            grad_query = None
            for b in range(a + 1):
                grad_score = (weights[b] * (slopes[b] - mean) * scaling).astype(BF16).astype(F32)
                term_q = grad_score * ks[b, r, c].astype(F32)
                term_k = grad_score * q
                term_v = rounded[b] * g
                grad_query = term_q if b == 0 else grad_query + term_q
                if a > b:
                    term_k = term_k + gk_sum[b, r, c]
                    term_v = term_v + gv_sum[b, r, c]
                if a == LV - 1:
                    gks[b, r, c] = term_k.astype(BF16)
                    gvs[b, r, c] = term_v.astype(BF16)
                else:
                    gk_sum[b, r, c] = term_k
                    gv_sum[b, r, c] = term_v
            gqs[a, r, c] = grad_query.astype(BF16)
            return carry

        lax.fori_loop(0, 16, attend_body, 0)

    def two_levels(first):
        x = normed[first : first + 2].reshape(2 * FR, WIDTH)
        for w, target in ((wq, qs), (wk, ks), (wv, vs)):
            target[first : first + 2] = dot(x, w[...]).astype(BF16).reshape(2, FR, COLS)
        count = 2 * (first + 1) + 2 * (first + 2)

        def product_body(i, carry):
            r = rows(i * 16, 16)
            base = 0
            for a in (first, first + 1):
                q = qs[a, r, :].astype(F32)
                g = gms[a, r, :].astype(F32)
                for b in range(a + 1):
                    prod[base + b, r, :] = (q * ks[b, r, :].astype(F32)).astype(BF16)
                    prod[base + a + 1 + b, r, :] = (g * vs[b, r, :].astype(F32)).astype(BF16)
                base += 2 * (a + 1)
            return carry

        lax.fori_loop(0, 8, product_body, 0)
        sums[0:count] = dot(prod[0:count].reshape(count * FR, COLS), same_head).reshape(count, FR, COLS)
        attend_level(first, 0)
        attend_level(first + 1, 2 * (first + 1))

    norm(0)
    norm(1)
    pass_stream(2)
    two_levels(0)
    norm(2)
    pass_stream(3)
    norm(3)
    two_levels(2)

    def stat_body(i, carry):
        r = rows(i * 32, 32)
        for k in range(LV):
            share = (
                qs[k, r, :].astype(F32) * gqs[k, r, :].astype(F32)
                + ks[k, r, :].astype(F32) * gks[k, r, :].astype(F32)
                + vs[k, r, :].astype(F32) * gvs[k, r, :].astype(F32)
            )
            stat_wide[k, r, :] = jnp.broadcast_to(jnp.sum(share, axis=1, keepdims=True), (32, 128))
        return carry

    lax.fori_loop(0, 4, stat_body, 0)
    eye = lax.broadcasted_iota(jnp.int32, (FR, FR), 0) == lax.broadcasted_iota(jnp.int32, (FR, FR), 1)
    for k in range(LV):
        stat[0, k : k + 1, :] = jnp.sum(jnp.where(eye, stat_wide[k], 0.0), axis=0, keepdims=True)
    stat[0, LV:, :] = jnp.zeros((8 - LV, FR), F32)
    stat_copies = [
        send(stat.at[0], stat.at[1], x_far),
        send(stat.at[0], stat.at[2], mate),
        send(stat.at[0], stat.at[3], cross),
    ]

    gq = gqs[...].reshape(LV * FR, COLS)
    gk = gks[...].reshape(LV * FR, COLS)
    gv = gvs[...].reshape(LV * FR, COLS)

    def partial(owner):
        w = rows(owner * COLS, COLS)
        total = dot_nt(gq, wq[w, :]) + dot_nt(gk, wk[w, :]) + dot_nt(gv, wv[w, :])
        return total.reshape(LV, FR, COLS)

    pn[0] = partial(lvl_cross).astype(BF16)
    pn_cross = [send(pn.at[0, k], pn_core.at[0, k], mate) for k in range(LV)]
    pn[2] = partial(lvl_far).astype(BF16)
    pn_far = []
    for k in range(LV):
        pn_cross[k].wait_recv()
        pn_mid[k] = (pn[2, k].astype(F32) + pn_core[0, k].astype(F32)).astype(BF16)
        pn_far.append(send(pn_mid.at[k], pn_x.at[k], x_far))
    pn[1] = partial(lvl_mate).astype(BF16)
    pn_mate = [send(pn.at[1, k], pn_core.at[1, k], mate) for k in range(LV)]
    opart[...] = dot(mix[...].reshape(LV * FR, COLS), wo[...]).astype(BF16).reshape(LV, FR, WIDTH)
    o_copies = [
        send(opart.at[:, cross_frames], o_core.at[0], mate),
        send(opart.at[:, mate_frames], o_core.at[1], mate),
    ]
    pn_own[...] = partial(lvl)

    for copy in stat_copies:
        copy.wait_recv()
    stat_all = (stat[0] + stat[1] + stat[2] + stat[3]) * (1.0 / WIDTH)
    for k in range(LV):
        column = jnp.sum(
            jnp.where(eye, jnp.broadcast_to(stat_all[k : k + 1, :], (FR, FR)), 0.0), axis=1, keepdims=True
        )
        stat_col[k] = jnp.broadcast_to(column, (FR, 128))

    own_cols = rows(lvl * COLS, COLS)
    gain = gain_ref[:, own_cols]
    context_grads = []
    g_copies = []

    def stream_grad(k):
        pn_mate[k].wait_recv()
        pn_far[k].wait_recv()
        grad_normed = pn_own[k] + pn_core[1, k].astype(F32) + pn_x[k].astype(F32)
        scaler = scale[k][:, 0:1]
        unit = stream_own[k] * scaler
        grad = ups[k, :, own_cols].astype(F32) + scaler * (gain * grad_normed - unit * stat_col[k][:, 0:1])
        context_grads.append(grad)
        eg[k, 0:FR, :] = (retain * grad if k == 0 else grad).astype(BF16)
        copies = []
        if k == LV - 1:
            copies.append(send(eg.at[k, 0:FR], eg.at[k, 3 * FR : 4 * FR], y_far))
        copies.append(send(eg.at[k, 0:FR], eg.at[k, FR : 2 * FR], y_up))
        copies.append(send(eg.at[k, 0:FR], eg.at[k, 2 * FR : 3 * FR], y_down))
        g_copies.append(copies)

    def pass_grad(k):
        copy_up, copy_down = g_copies[k]
        copy_up.wait_recv()
        pass_up = send(eg.at[k, FR : FR + FR // 2], eg.at[k, 3 * FR : 3 * FR + FR // 2], y_up)
        copy_down.wait_recv()
        pass_down = send(
            eg.at[k, 2 * FR + FR // 2 : 3 * FR], eg.at[k, 3 * FR + FR // 2 : 4 * FR], y_down
        )
        g_copies[k] = [pass_up, pass_down]

    stream_grad(0)
    stream_grad(1)
    o_copies[0].wait_recv()
    o_mid[...] = (opart[:, far_frames, :].astype(F32) + o_core[0].astype(F32)).astype(BF16)
    stream_grad(2)
    o_far = send(o_mid, o_x, x_far)
    pass_grad(0)
    stream_grad(3)
    pass_grad(1)
    cgs[lvl] = (context_grads[0] + context_grads[1] + context_grads[2] + context_grads[3]).astype(BF16)
    cg_far = push(cgs.at[lvl], x_far)
    cg_mate = push(cgs.at[lvl], mate)
    pass_grad(2)

    half = ENT // 2
    fringe, crossed, direct_sums = [], [], []

    def packed(xx, zz, k):
        return grads[k, block_rows(xx, zz), :]

    def fringe_step(k):
        for copy in g_copies[k]:
            copy.wait_recv()
        grads[k] = dot(oht[k], eg[k])
        for j, xx in enumerate((xl, 1 - xl)):
            f3_send[0, k, j] = packed(xx, z - 3, k).astype(BF16)
            f3_send[1, k, j] = packed(xx, z + 3, k).astype(BF16)
            value = packed(xx, z + 4, k).astype(BF16)
            f4_send[0, k, j] = value[0:half, :]
            f4_send[1, k, j] = value[half:, :]
        fringe.append(
            [
                send(f3_send.at[0, k], f3_recv.at[0, k], z_down),
                send(f3_send.at[1, k], f3_recv.at[1, k], z_up),
                send(f4_send.at[0, k], f4_recv.at[0, k], z_down2),
                send(f4_send.at[1, k], f4_recv.at[1, k], z_up2),
            ]
        )
        for o in range(3):
            c1_send[k, o] = packed(1 - xl, z + o - 1, k).astype(BF16)
        crossed.append([send(c1_send.at[k], c1_recv.at[k], x_near)])

    def two_away(side, j, k):
        value = packed(xl if j == 0 else 1 - xl, z - 2 if side == 0 else z + 2, k)
        value = value + f3_recv[side, k, j].astype(F32)
        ends = f4_recv[side, k, j].astype(F32)
        zeros = jnp.zeros((half, COLS), F32)
        return value + jnp.concatenate([ends, zeros] if side == 0 else [zeros, ends], axis=0)

    def cross_step(k):
        for copy in fringe[k]:
            copy.wait_recv()
        for side in range(2):
            c2_send[k, side] = two_away(side, 1, k).astype(BF16)
        crossed[k].append(send(c2_send.at[k], c2_recv.at[k], x_near))

    def direct_step(k):
        for copy in crossed[k]:
            copy.wait_recv()
        for side in range(2):
            value = two_away(side, 0, k) + c2_recv[k, side].astype(F32)
            d_send[2 + side, k] = value.astype(BF16)
            value = packed(xl, z + 2 * side - 1, k) + c1_recv[k, 2 * side].astype(F32)
            d_send[side, k] = value.astype(BF16)
        direct_sums.append(
            [
                send(d_send.at[i, k], d_recv.at[i, k], target)
                for i, target in ((2, z_down2), (3, z_up2), (0, z_down), (1, z_up))
            ]
        )

    def final_step(k):
        value = packed(xl, z, k) + c1_recv[k, 1].astype(F32)
        for copy in direct_sums[k]:
            copy.wait_recv()
        for i in range(4):
            value = value + d_recv[i, k].astype(F32)
        tg_ref[k] = value

    fringe_step(0)
    fringe_step(1)
    fringe_step(2)
    fringe_step(3)
    cross_step(0)
    cross_step(1)
    direct_step(0)
    cross_step(2)
    cross_step(3)
    cg_far.wait_recv()
    cg_pass = push(cgs.at[lvl_far], mate)
    direct_step(1)
    direct_step(2)
    direct_step(3)

    cg_mate.wait_recv()
    cg_pass.wait_recv()
    whole = jnp.concatenate([cgs[b] for b in range(4)], axis=1)
    hg_ref[...] = dot_nt(whole, win[...]).astype(BF16)

    o_copies[1].wait_recv()
    o_far.wait_recv()
    for k in range(LV):
        base = jnp.concatenate([streams[b, k, own_frames, :] for b in range(4)], axis=1).astype(F32)
        out_ref[k] = (
            base + opart[k, own_frames, :].astype(F32) + o_core[1, k].astype(F32) + o_x[k].astype(F32)
        ).astype(BF16)
    for k in range(LV):
        final_step(k)

    for copy in started:
        copy.wait_send()
    assert len(started) <= COPIES


def shards(
    hidden, code_ids, lengths, weight_in, weight_query, weight_key, weight_value, weight_out,
    norm_gain, tables, upstream,
):
    vmem = pl.BlockSpec(memory_space=pltpu.VMEM)
    hbm = pl.BlockSpec(memory_space=pltpu.HBM)

    def scratch(dtype, *shape):
        return pltpu.VMEM(shape, dtype)

    block = (LV, FR, COLS)
    out, hidden_grad, table_grad = pl.pallas_call(
        kernel,
        out_shape=(
            jax.ShapeDtypeStruct((LV, OWN, WIDTH), BF16),
            jax.ShapeDtypeStruct((FR, WIDTH), BF16),
            jax.ShapeDtypeStruct((LV, ENT, COLS), F32),
        ),
        in_specs=[hbm] * 11,
        out_specs=(vmem, vmem, vmem),
        scratch_shapes=[
            scratch(jnp.int32, 8, FR),
            pltpu.SMEM((4,), jnp.int32),
            scratch(F32, 1, WIDTH),
            scratch(BF16, FR, WIDTH),
            scratch(BF16, WIDTH, WIDTH),
            scratch(BF16, WIDTH, COLS),
            scratch(BF16, WIDTH, COLS),
            scratch(BF16, WIDTH, COLS),
            scratch(BF16, COLS, WIDTH),
            scratch(jnp.int32, 8, FR),
            scratch(jnp.int32, NY, 8, FR),
            scratch(BF16, LV, RANGE, COLS),
            scratch(BF16, LV, NY * FR, RANGE),
            scratch(BF16, LV, RANGE, NY * FR),
            scratch(BF16, LV, FR, WIDTH),
            scratch(BF16, 4, FR, COLS),
            scratch(BF16, 2, FR, COLS),
            scratch(BF16, FR, COLS),
            scratch(BF16, FR, COLS),
            scratch(BF16, NY, *block),
            scratch(BF16, 2, LV, FR // 2, COLS),
            scratch(BF16, 2, *block),
            scratch(F32, *block),
            scratch(BF16, 4, *block),
            scratch(BF16, LV, FR, WIDTH),
            scratch(F32, LV, FR, 128),
            scratch(BF16, *block),
            scratch(BF16, *block),
            scratch(BF16, *block),
            scratch(BF16, *block),
            scratch(BF16, 14, FR, COLS),
            scratch(F32, 14, FR, COLS),
            scratch(BF16, *block),
            scratch(BF16, *block),
            scratch(BF16, *block),
            scratch(BF16, *block),
            scratch(F32, *block),
            scratch(F32, *block),
            scratch(BF16, 3, *block),
            scratch(F32, *block),
            scratch(BF16, 2, *block),
            scratch(BF16, *block),
            scratch(BF16, *block),
            scratch(F32, LV, FR, 128),
            scratch(F32, 4, 8, FR),
            scratch(F32, LV, FR, 128),
            scratch(BF16, LV, FR, WIDTH),
            scratch(BF16, 2, LV, OWN, WIDTH),
            scratch(BF16, LV, OWN, WIDTH),
            scratch(BF16, LV, OWN, WIDTH),
            scratch(BF16, LV, NY * FR, COLS),
            scratch(BF16, 4, FR, COLS),
            scratch(F32, LV, RANGE, COLS),
            scratch(BF16, 2, LV, 2, ENT, COLS),
            scratch(BF16, 2, LV, 2, ENT, COLS),
            scratch(BF16, 2, LV, 2, ENT // 2, COLS),
            scratch(BF16, 2, LV, 2, ENT // 2, COLS),
            scratch(BF16, LV, 3, ENT, COLS),
            scratch(BF16, LV, 3, ENT, COLS),
            scratch(BF16, LV, 2, ENT, COLS),
            scratch(BF16, LV, 2, ENT, COLS),
            scratch(BF16, 4, LV, ENT, COLS),
            scratch(BF16, 4, LV, ENT, COLS),
            pltpu.SemaphoreType.DMA((11,)),
            pltpu.SemaphoreType.DMA((COPIES,)),
            pltpu.SemaphoreType.DMA((COPIES,)),
        ],
        compiler_params=pltpu.CompilerParams(
            collective_id=0, has_side_effects=True, vmem_limit_bytes=53 << 20
        ),
        name="layer",
    )(
        code_ids.T,
        lengths,
        norm_gain.reshape(1, WIDTH),
        jnp.transpose(tables, (1, 0, 2)),
        jnp.transpose(upstream, (1, 0, 2)),
        hidden,
        weight_in,
        weight_query,
        weight_key,
        weight_value,
        weight_out,
    )
    return (
        jnp.transpose(out, (1, 0, 2)),
        hidden_grad,
        jnp.transpose(table_grad, (1, 0, 2)),
    )


def solution(mesh):
    placed = (
        P("seq", "lvl"),
        P("seq", None),
        P(),
        P("lvl", None),
        P(None, "lvl"),
        P(None, "lvl"),
        P(None, "lvl"),
        P("lvl", None),
        P(),
        P("seq", None, "lvl"),
        P(("seq", "lvl"), None, None),
    )
    return jax.shard_map(
        shards,
        mesh=mesh,
        in_specs=placed,
        out_specs=(P(("seq", "lvl"), None, None), P("seq", "lvl"), P("seq", None, "lvl")),
        check_vma=False,
    )
```

```python
import math

import jax
import jax.numpy as jnp
from jax import lax
from jax.experimental import pallas as pl
from jax.experimental.pallas import tpu as pltpu
from jax.sharding import PartitionSpec as P

HEADS = 16
EPSILON = 1e-05
MESH = pl.DeviceIdType.MESH
F32 = jnp.float32
BF16 = jnp.bfloat16

NY, NZ = 4, 8
LV = 4
FR = 128
OWN = 32
COLS = 256
WIDTH = 1024
ENT = 32
RANGE = 512
COPIES = 192
VMEM_BYTES = 56 << 20


def dot(a, b):
    return lax.dot_general(a, b, (((1,), (0,)), ((), ())), preferred_element_type=F32)


def dot_nt(a, b):
    return lax.dot_general(a, b, (((1,), (1,)), ((), ())), preferred_element_type=F32)


def kernel(
    codes_hbm, lens_hbm, gain_hbm, tab_hbm, up_hbm, hid_hbm, win_hbm, wq_hbm, wk_hbm, wv_hbm, wo_hbm,
    out_hbm, hg_hbm, tg_hbm,
    out_ref, hg_ref, tg_ref,
    tab_in, up_in, codes_ref, lens_ref, gain_ref, hid_ref, win, wq, wk, wv, wo,
    nbr, prev, tab, oh, oht, ups, ctx_send, ctx_core, ctx_mid, ctx_x,
    look, relay, fin, stream_own, streams, normed, scale,
    qs, ks, vs, gms, prod, sums, mix, gqs, gks, gvs, gk_sum, gv_sum,
    pn, pn_own, pn_core, pn_mid, pn_x, stat_wide, stat, stat_col,
    opart, o_core, o_mid, o_x,
    eg, cgs, grads, f3_send, f3_recv, f4_send, f4_recv, c1_send, c1_recv, c2_send, c2_recv, d_send, d_recv,
    local_sem, ssem, rsem,
):
    seq = lax.axis_index("seq")
    lvl = lax.axis_index("lvl")
    y = lax.div(seq, 16)
    xl = lax.rem(lax.div(seq, 8), 2)
    z = lax.rem(seq, 8)
    xh = lax.div(lvl, 2)
    core = lax.rem(lvl, 2)

    def device(dy=0, dx=0, dz=0, dh=0, dc=0):
        yy = lax.rem(y + dy + NY, NY)
        xx = 1 - xl if dx else xl
        zz = lax.rem(z + dz + NZ, NZ)
        hh = 1 - xh if dh else xh
        cc = 1 - core if dc else core
        return (yy * 16 + xx * 8 + zz, hh * 2 + cc)

    seq_next = (lax.rem(seq + 1, 64), lvl)
    seq_back = (lax.rem(seq + 63, 64), lvl)
    y_up, y_down, y_far = device(dy=1), device(dy=-1), device(dy=2)
    z_up, z_down, z_up2, z_down2 = device(dz=1), device(dz=-1), device(dz=2), device(dz=-2)
    x_near, x_far, mate, cross = device(dx=1), device(dh=1), device(dc=1), device(dh=1, dc=1)
    lvl_far = (1 - xh) * 2 + core
    lvl_mate = xh * 2 + 1 - core
    lvl_cross = (1 - xh) * 2 + 1 - core

    started = []

    def send(src, dst, target):
        i = len(started)
        copy = pltpu.make_async_remote_copy(
            src_ref=src, dst_ref=dst, send_sem=ssem.at[i], recv_sem=rsem.at[i],
            device_id=target, device_id_type=MESH,
        )
        copy.start()
        started.append(copy)
        return copy

    def push(ref, target):
        return send(ref, ref, target)

    def rows(start, size):
        return pl.ds(pl.multiple_of(start, size), size)

    def block_rows(xx, zz):
        return rows((xx * 8 + lax.rem(zz + NZ, NZ)) * ENT, ENT)

    own_rows = block_rows(xl, z)
    own_frames = rows(lvl * OWN, OWN)
    far_frames = rows(lvl_far * OWN, OWN)
    mate_frames = rows(lvl_mate * OWN, OWN)
    cross_frames = rows(lvl_cross * OWN, OWN)

    codes_ref[...] = jnp.zeros((8, FR), jnp.int32)
    fetch = {}
    for i, (name, a, b) in enumerate(
        (
            ("tab", tab_hbm, tab_in),
            ("codes", codes_hbm, codes_ref.at[0:LV]),
            ("hid", hid_hbm, hid_ref),
            ("win", win_hbm, win),
            ("ups", up_hbm, up_in),
            ("lens", lens_hbm, lens_ref),
            ("gain", gain_hbm, gain_ref),
            ("wo", wo_hbm, wo),
            ("wq", wq_hbm, wq),
            ("wk", wk_hbm, wk),
            ("wv", wv_hbm, wv),
        )
    ):
        fetch[name] = pltpu.make_async_copy(a, b, local_sem.at[i])
        fetch[name].start()

    barrier = pltpu.get_barrier_semaphore()
    for source in (z_up, z_down, z_up2, z_down2, x_near, y_up, y_down, y_far, mate, x_far, cross, seq_back):
        pl.semaphore_signal(barrier, inc=1, device_id=source, device_id_type=MESH)
    fetch["hid"].wait()
    fetch["win"].wait()
    part = dot(hid_ref[...], win[...])
    for b in range(4):
        ctx_send[b] = part[:, b * COLS : (b + 1) * COLS].astype(BF16)
    fetch["tab"].wait()
    for k in range(LV):
        tab[k, own_rows, :] = tab_in[:, k, :]
    fetch["codes"].wait()
    pl.semaphore_wait(barrier, 12)

    def block(half, xx, zz):
        return tab.at[2 * half : 2 * half + 2, block_rows(xx, zz)]

    own = [block(h, xl, z) for h in range(2)]
    up2, down2, up1, down1, near_own = [], [], [], [], []
    for h in range(2):
        up2.append(push(own[h], z_up2))
        down2.append(push(own[h], z_down2))
        near_own.append(push(own[h], x_near))
        up1.append(push(own[h], z_up))
        down1.append(push(own[h], z_down))
    code_copy = send(codes_ref, nbr, seq_next)
    ctx_copies = [
        send(ctx_send.at[lvl_cross], ctx_core.at[0], mate),
        send(ctx_send.at[lvl_mate], ctx_core.at[1], mate),
    ]
    fetch["ups"].wait()
    for k in range(LV):
        ups[k, own_frames, :] = up_in[:, k, :]
    up_mate = [push(ups.at[k, own_frames], mate) for k in range(LV)]

    near2, up3, down3, near1 = [], [], [], []
    for h in range(2):
        up2[h].wait_recv()
        near2.append(push(block(h, xl, z - 2), x_near))
        up3.append(push(block(h, xl, z - 2), z_up))
        if h == 0:
            end_up = push(block(0, xl, z - 2), z_up2)
        down2[h].wait_recv()
        near2.append(push(block(h, xl, z + 2), x_near))
        down3.append(push(block(h, xl, z + 2), z_down))
        if h == 1:
            end_down = push(block(1, xl, z + 2), z_down2)
    for h in range(2):
        up1[h].wait_recv()
        near1.append(push(block(h, xl, z - 1), x_near))
        down1[h].wait_recv()
        near1.append(push(block(h, xl, z + 1), x_near))

    code_copy.wait_recv()
    lane8 = lax.broadcasted_iota(jnp.int32, (8, FR), 1)
    sub8 = lax.broadcasted_iota(jnp.int32, (8, FR), 0)
    own_codes = codes_ref[...]
    shifted = pltpu.roll(own_codes, 1, 1)
    incoming = pltpu.roll(nbr[...], 1, 1)
    incoming = jnp.where(jnp.broadcast_to(seq, (8, FR)) == 0, 0, incoming)
    shifted = jnp.where(lane8 == 0, incoming, shifted)
    first_row = jnp.broadcast_to(shifted[LV - 1 : LV, :], (8, FR))
    prev[0] = jnp.where(sub8 == 0, first_row, pltpu.roll(own_codes, 1, 0))
    code_y = [
        send(prev.at[0], prev.at[1], y_up),
        send(prev.at[0], prev.at[2], y_down),
        send(prev.at[0], prev.at[3], y_far),
    ]
    ctx_copies[0].wait_recv()
    ctx_mid[...] = (ctx_send[lvl_far].astype(F32) + ctx_core[0].astype(F32)).astype(BF16)
    ctx_far = send(ctx_mid, ctx_x, x_far)

    for copy in code_y:
        copy.wait_recv()
    first = y * RANGE
    by_lane = lax.broadcasted_iota(jnp.int32, (FR, RANGE), 1) + first
    by_row = lax.broadcasted_iota(jnp.int32, (RANGE, FR), 0) + first
    for slot in range(NY):
        codes = prev[slot]
        turned = jnp.transpose(
            jnp.concatenate([codes.astype(F32), jnp.zeros((FR - 8, FR), F32)], axis=0)
        ).astype(jnp.int32)
        for k in range(LV):
            column = jnp.broadcast_to(turned[:, k : k + 1], (FR, RANGE))
            oh[k, slot * FR : (slot + 1) * FR, :] = jnp.where(column == by_lane, 1.0, 0.0).astype(BF16)

    far_up, far_down = [], []
    for h in range(2):
        near2[2 * h].wait_recv()
        far_up.append(push(block(h, 1 - xl, z - 2), z_up))
        if h == 0:
            far_end_up = push(block(0, 1 - xl, z - 2), z_up2)
        near2[2 * h + 1].wait_recv()
        far_down.append(push(block(h, 1 - xl, z + 2), z_down))
        if h == 1:
            far_end_down = push(block(1, 1 - xl, z + 2), z_down2)
    up_far = [push(ups.at[k, own_frames], x_far) for k in range(LV)]

    for slot in range(NY):
        codes = prev[slot]
        for k in range(LV):
            row = jnp.broadcast_to(codes[k : k + 1, :], (RANGE, FR))
            oht[k, :, slot * FR : (slot + 1) * FR] = jnp.where(row == by_row, 1.0, 0.0).astype(BF16)
    fetch["lens"].wait()
    frame = lax.broadcasted_iota(jnp.int32, (FR, COLS), 0) + seq * FR
    begin = jnp.int32(0)
    retain = jnp.ones((FR, COLS), F32)
    for i in range(4):
        retain = jnp.where(frame == begin, 0.0, retain)
        begin = begin + lens_ref[i]
    ctx_copies[1].wait_recv()
    ctx_far.wait_recv()
    context = ctx_send[lvl].astype(F32) + ctx_core[1].astype(F32) + ctx_x[...].astype(F32)

    top, low = slice(0, FR // 2), slice(FR // 2, FR)
    relay_up, relay_down = [], []
    fin_up = [[None, None] for _ in range(LV)]
    fin_down = [[None, None] for _ in range(LV)]

    def find(k):
        found = dot(oh[k], tab[k]).astype(BF16)
        for slot in (3, 2, 1, 0):
            look[slot, k] = found[slot * FR : (slot + 1) * FR, :]
        relay_up.append(send(look.at[3, k, top], relay.at[0, k], y_up))
        relay_down.append(send(look.at[3, k, low], relay.at[1, k], y_down))

    def direct(k):
        fin_up[k][1] = send(look.at[2, k, low], fin.at[0, k, low], y_up)
        fin_down[k][0] = send(look.at[1, k, top], fin.at[1, k, top], y_down)

    def relayed(k):
        relay_up[k].wait_recv()
        look[2, k, top] = look[2, k, top] + relay[0, k]
        fin_up[k][0] = send(look.at[2, k, top], fin.at[0, k, top], y_up)
        relay_down[k].wait_recv()
        look[1, k, low] = look[1, k, low] + relay[1, k]
        fin_down[k][1] = send(look.at[1, k, low], fin.at[1, k, low], y_down)

    far, near, passed = [], [], []

    def stream(k):
        for copy in fin_up[k] + fin_down[k]:
            copy.wait_recv()
        embedded = look[0, k].astype(F32) + fin[0, k].astype(F32) + fin[1, k].astype(F32)
        if k == 0:
            embedded = retain * embedded
        own = context + embedded
        stream_own[k] = own
        streams[lvl, k] = own.astype(BF16)
        far.append(push(streams.at[lvl, k], x_far))
        near.append(push(streams.at[lvl, k], mate))

    def pass_stream(k):
        far[k].wait_recv()
        passed.append(push(streams.at[lvl_far, k], mate))

    def blocks_in(h):
        for copy in (up3[h], down3[h], near_own[h], near1[2 * h], near1[2 * h + 1], far_up[h], far_down[h]):
            copy.wait_recv()

    blocks_in(0)
    end_up.wait_recv()
    far_end_up.wait_recv()
    find(0)
    find(1)
    direct(0)
    blocks_in(1)
    end_down.wait_recv()
    far_end_down.wait_recv()
    find(2)
    find(3)
    direct(1)
    relayed(0)
    relayed(1)
    direct(2)
    relayed(2)
    direct(3)
    relayed(3)
    stream(0)
    stream(1)
    stream(2)
    stream(3)
    up_pass = []
    for k in range(LV):
        up_far[k].wait_recv()
        up_pass.append(push(ups.at[k, far_frames], mate))
    pass_stream(0)
    pass_stream(1)
    fetch["wo"].wait()
    for k in range(LV):
        up_mate[k].wait_recv()
        up_pass[k].wait_recv()
    gms[...] = dot_nt(ups[...].reshape(LV * FR, WIDTH), wo[...]).astype(BF16).reshape(LV, FR, COLS)
    for name in ("gain", "wq", "wk", "wv"):
        fetch[name].wait()

    head_row = lax.shift_right_logical(lax.broadcasted_iota(jnp.int32, (COLS, COLS), 0), 6)
    head_col = lax.shift_right_logical(lax.broadcasted_iota(jnp.int32, (COLS, COLS), 1), 6)
    same_head = jnp.where(head_row == head_col, 1.0, 0.0).astype(BF16)
    scaling = 1.0 / math.sqrt(WIDTH // HEADS)

    def norm(a):
        near[a].wait_recv()
        passed[a].wait_recv()

        def norm_body(i, carry):
            r = rows(i * 32, 32)
            blocks = [streams[b, a, r, :].astype(F32) for b in range(4)]
            total = blocks[0] * blocks[0]
            for b in range(1, 4):
                total = total + blocks[b] * blocks[b]
            scaler = lax.rsqrt(jnp.sum(total, axis=1, keepdims=True) * (1.0 / WIDTH) + EPSILON)
            scale[a, r, :] = jnp.broadcast_to(scaler, (32, 128))
            for b in range(4):
                normed[a, r, b * COLS : (b + 1) * COLS] = (
                    blocks[b] * scaler * gain_ref[:, b * COLS : (b + 1) * COLS]
                ).astype(BF16)
            return carry

        lax.fori_loop(0, 4, norm_body, 0)

    def attend_level(a, base):
        def attend_body(i, carry):
            r = rows(lax.div(i, 2) * 16, 16)
            c = rows(lax.rem(i, 2) * 128, 128)
            q = qs[a, r, c].astype(F32)
            g = gms[a, r, c].astype(F32)
            raised = [jnp.exp(sums[base + b, r, c] * scaling) for b in range(a + 1)]
            total = raised[0]
            for b in range(1, a + 1):
                total = total + raised[b]
            inverse = 1.0 / total
            weights = [x * inverse for x in raised]
            rounded = [x.astype(BF16).astype(F32) for x in weights]
            slopes = [sums[base + a + 1 + b, r, c] for b in range(a + 1)]
            mixed = rounded[0] * vs[0, r, c].astype(F32)
            mean = weights[0] * slopes[0]
            for b in range(1, a + 1):
                mixed = mixed + rounded[b] * vs[b, r, c].astype(F32)
                mean = mean + weights[b] * slopes[b]
            mix[a, r, c] = mixed.astype(BF16)
            grad_query = None
            for b in range(a + 1):
                grad_score = (weights[b] * (slopes[b] - mean) * scaling).astype(BF16).astype(F32)
                term_q = grad_score * ks[b, r, c].astype(F32)
                term_k = grad_score * q
                term_v = rounded[b] * g
                grad_query = term_q if b == 0 else grad_query + term_q
                if a > b:
                    term_k = term_k + gk_sum[b, r, c]
                    term_v = term_v + gv_sum[b, r, c]
                if a == LV - 1:
                    gks[b, r, c] = term_k.astype(BF16)
                    gvs[b, r, c] = term_v.astype(BF16)
                else:
                    gk_sum[b, r, c] = term_k
                    gv_sum[b, r, c] = term_v
            gqs[a, r, c] = grad_query.astype(BF16)
            return carry

        lax.fori_loop(0, 16, attend_body, 0)

    def two_levels(first):
        x = normed[first : first + 2].reshape(2 * FR, WIDTH)
        for w, target in ((wq, qs), (wk, ks), (wv, vs)):
            target[first : first + 2] = dot(x, w[...]).astype(BF16).reshape(2, FR, COLS)
        count = 2 * (first + 1) + 2 * (first + 2)

        def product_body(i, carry):
            r = rows(i * 16, 16)
            base = 0
            for a in (first, first + 1):
                q = qs[a, r, :].astype(F32)
                g = gms[a, r, :].astype(F32)
                for b in range(a + 1):
                    prod[base + b, r, :] = (q * ks[b, r, :].astype(F32)).astype(BF16)
                    prod[base + a + 1 + b, r, :] = (g * vs[b, r, :].astype(F32)).astype(BF16)
                base += 2 * (a + 1)
            return carry

        lax.fori_loop(0, 8, product_body, 0)
        sums[0:count] = dot(prod[0:count].reshape(count * FR, COLS), same_head).reshape(count, FR, COLS)
        attend_level(first, 0)
        attend_level(first + 1, 2 * (first + 1))

    norm(0)
    norm(1)
    pass_stream(2)
    two_levels(0)
    norm(2)
    pass_stream(3)
    norm(3)
    two_levels(2)

    def stat_body(i, carry):
        r = rows(i * 32, 32)
        for k in range(LV):
            share = (
                qs[k, r, :].astype(F32) * gqs[k, r, :].astype(F32)
                + ks[k, r, :].astype(F32) * gks[k, r, :].astype(F32)
                + vs[k, r, :].astype(F32) * gvs[k, r, :].astype(F32)
            )
            stat_wide[k, r, :] = jnp.broadcast_to(jnp.sum(share, axis=1, keepdims=True), (32, 128))
        return carry

    lax.fori_loop(0, 4, stat_body, 0)
    eye = lax.broadcasted_iota(jnp.int32, (FR, FR), 0) == lax.broadcasted_iota(jnp.int32, (FR, FR), 1)
    for k in range(LV):
        stat[0, k : k + 1, :] = jnp.sum(jnp.where(eye, stat_wide[k], 0.0), axis=0, keepdims=True)
    stat[0, LV:, :] = jnp.zeros((8 - LV, FR), F32)
    stat_copies = [
        send(stat.at[0], stat.at[1], x_far),
        send(stat.at[0], stat.at[2], mate),
        send(stat.at[0], stat.at[3], cross),
    ]

    gq = gqs[...].reshape(LV * FR, COLS)
    gk = gks[...].reshape(LV * FR, COLS)
    gv = gvs[...].reshape(LV * FR, COLS)

    def partial(owner):
        w = rows(owner * COLS, COLS)
        total = dot_nt(gq, wq[w, :]) + dot_nt(gk, wk[w, :]) + dot_nt(gv, wv[w, :])
        return total.reshape(LV, FR, COLS)

    pn[0] = partial(lvl_cross).astype(BF16)
    pn_cross = [send(pn.at[0, k], pn_core.at[0, k], mate) for k in range(LV)]
    pn[2] = partial(lvl_far).astype(BF16)
    pn_far = []
    for k in range(LV):
        pn_cross[k].wait_recv()
        pn_mid[k] = (pn[2, k].astype(F32) + pn_core[0, k].astype(F32)).astype(BF16)
        pn_far.append(send(pn_mid.at[k], pn_x.at[k], x_far))
    pn[1] = partial(lvl_mate).astype(BF16)
    pn_mate = [send(pn.at[1, k], pn_core.at[1, k], mate) for k in range(LV)]
    opart[...] = dot(mix[...].reshape(LV * FR, COLS), wo[...]).astype(BF16).reshape(LV, FR, WIDTH)
    o_copies = [
        send(opart.at[:, cross_frames], o_core.at[0], mate),
        send(opart.at[:, mate_frames], o_core.at[1], mate),
    ]
    pn_own[...] = partial(lvl)

    for copy in stat_copies:
        copy.wait_recv()
    stat_all = (stat[0] + stat[1] + stat[2] + stat[3]) * (1.0 / WIDTH)
    for k in range(LV):
        column = jnp.sum(
            jnp.where(eye, jnp.broadcast_to(stat_all[k : k + 1, :], (FR, FR)), 0.0), axis=1, keepdims=True
        )
        stat_col[k] = jnp.broadcast_to(column, (FR, 128))

    own_cols = rows(lvl * COLS, COLS)
    gain = gain_ref[:, own_cols]
    context_grads = []
    g_copies = []

    def stream_grad(k):
        pn_mate[k].wait_recv()
        pn_far[k].wait_recv()
        grad_normed = pn_own[k] + pn_core[1, k].astype(F32) + pn_x[k].astype(F32)
        scaler = scale[k][:, 0:1]
        unit = stream_own[k] * scaler
        grad = ups[k, :, own_cols].astype(F32) + scaler * (gain * grad_normed - unit * stat_col[k][:, 0:1])
        context_grads.append(grad)
        eg[k, 0:FR, :] = (retain * grad if k == 0 else grad).astype(BF16)
        copies = []
        if k == LV - 1:
            copies.append(send(eg.at[k, 0:FR], eg.at[k, 3 * FR : 4 * FR], y_far))
        copies.append(send(eg.at[k, 0:FR], eg.at[k, FR : 2 * FR], y_up))
        copies.append(send(eg.at[k, 0:FR], eg.at[k, 2 * FR : 3 * FR], y_down))
        g_copies.append(copies)

    def pass_grad(k):
        copy_up, copy_down = g_copies[k]
        copy_up.wait_recv()
        pass_up = send(eg.at[k, FR : FR + FR // 2], eg.at[k, 3 * FR : 3 * FR + FR // 2], y_up)
        copy_down.wait_recv()
        pass_down = send(
            eg.at[k, 2 * FR + FR // 2 : 3 * FR], eg.at[k, 3 * FR + FR // 2 : 4 * FR], y_down
        )
        g_copies[k] = [pass_up, pass_down]

    stream_grad(0)
    stream_grad(1)
    o_copies[0].wait_recv()
    o_mid[...] = (opart[:, far_frames, :].astype(F32) + o_core[0].astype(F32)).astype(BF16)
    stream_grad(2)
    o_far = send(o_mid, o_x, x_far)
    pass_grad(0)
    stream_grad(3)
    pass_grad(1)
    cgs[lvl] = (context_grads[0] + context_grads[1] + context_grads[2] + context_grads[3]).astype(BF16)
    cg_far = push(cgs.at[lvl], x_far)
    cg_mate = push(cgs.at[lvl], mate)
    pass_grad(2)

    half = ENT // 2
    fringe, crossed, direct_sums = [], [], []

    def packed(xx, zz, k):
        return grads[k, block_rows(xx, zz), :]

    def fringe_step(k):
        for copy in g_copies[k]:
            copy.wait_recv()
        grads[k] = dot(oht[k], eg[k])
        for j, xx in enumerate((xl, 1 - xl)):
            f3_send[0, k, j] = packed(xx, z - 3, k).astype(BF16)
            f3_send[1, k, j] = packed(xx, z + 3, k).astype(BF16)
            value = packed(xx, z + 4, k).astype(BF16)
            f4_send[0, k, j] = value[0:half, :]
            f4_send[1, k, j] = value[half:, :]
        fringe.append(
            [
                send(f3_send.at[0, k], f3_recv.at[0, k], z_down),
                send(f3_send.at[1, k], f3_recv.at[1, k], z_up),
                send(f4_send.at[0, k], f4_recv.at[0, k], z_down2),
                send(f4_send.at[1, k], f4_recv.at[1, k], z_up2),
            ]
        )
        for o in range(3):
            c1_send[k, o] = packed(1 - xl, z + o - 1, k).astype(BF16)
        crossed.append([send(c1_send.at[k], c1_recv.at[k], x_near)])

    def two_away(side, j, k):
        value = packed(xl if j == 0 else 1 - xl, z - 2 if side == 0 else z + 2, k)
        value = value + f3_recv[side, k, j].astype(F32)
        ends = f4_recv[side, k, j].astype(F32)
        zeros = jnp.zeros((half, COLS), F32)
        return value + jnp.concatenate([ends, zeros] if side == 0 else [zeros, ends], axis=0)

    def cross_step(k):
        for copy in fringe[k]:
            copy.wait_recv()
        for side in range(2):
            c2_send[k, side] = two_away(side, 1, k).astype(BF16)
        crossed[k].append(send(c2_send.at[k], c2_recv.at[k], x_near))

    def direct_step(k):
        for copy in crossed[k]:
            copy.wait_recv()
        for side in range(2):
            value = two_away(side, 0, k) + c2_recv[k, side].astype(F32)
            d_send[2 + side, k] = value.astype(BF16)
            value = packed(xl, z + 2 * side - 1, k) + c1_recv[k, 2 * side].astype(F32)
            d_send[side, k] = value.astype(BF16)
        direct_sums.append(
            [
                send(d_send.at[i, k], d_recv.at[i, k], target)
                for i, target in ((2, z_down2), (3, z_up2), (0, z_down), (1, z_up))
            ]
        )

    def final_step(k):
        value = packed(xl, z, k) + c1_recv[k, 1].astype(F32)
        for copy in direct_sums[k]:
            copy.wait_recv()
        for i in range(4):
            value = value + d_recv[i, k].astype(F32)
        tg_ref[:, k, :] = value

    fringe_step(0)
    fringe_step(1)
    fringe_step(2)
    fringe_step(3)
    cross_step(0)
    cross_step(1)
    direct_step(0)
    cross_step(2)
    cross_step(3)
    cg_far.wait_recv()
    cg_pass = push(cgs.at[lvl_far], mate)
    direct_step(1)
    direct_step(2)
    direct_step(3)

    cg_mate.wait_recv()
    cg_pass.wait_recv()
    whole = jnp.concatenate([cgs[b] for b in range(4)], axis=1)
    hg_ref[...] = dot_nt(whole, win[...]).astype(BF16)
    hg_copy = pltpu.make_async_copy(hg_ref, hg_hbm, local_sem.at[11])
    hg_copy.start()

    o_copies[1].wait_recv()
    o_far.wait_recv()
    for k in range(LV):
        base = jnp.concatenate([streams[b, k, own_frames, :] for b in range(4)], axis=1).astype(F32)
        out_ref[:, k, :] = (
            base + opart[k, own_frames, :].astype(F32) + o_core[1, k].astype(F32) + o_x[k].astype(F32)
        ).astype(BF16)
    out_copy = pltpu.make_async_copy(out_ref, out_hbm, local_sem.at[12])
    out_copy.start()
    for k in range(LV):
        final_step(k)
    tg_copy = pltpu.make_async_copy(tg_ref, tg_hbm, local_sem.at[13])
    tg_copy.start()

    for copy in started:
        copy.wait_send()
    for copy in (hg_copy, out_copy, tg_copy):
        copy.wait()
    assert len(started) <= COPIES


def hand_over(out_in, hg_in, tg_in, out_ref, hg_ref, tg_ref, out_held, hg_held, tg_held, sem):
    held = (out_held, hg_held, tg_held)
    first = [
        pltpu.make_async_copy(a, b, sem.at[i]) for i, (a, b) in enumerate(zip((out_in, hg_in, tg_in), held))
    ]
    second = [
        pltpu.make_async_copy(a, b, sem.at[3 + i])
        for i, (a, b) in enumerate(zip(held, (out_ref, hg_ref, tg_ref)))
    ]
    for copy in first:
        copy.start()
    for before, after in zip(first, second):
        before.wait()
        after.start()
    for copy in second:
        copy.wait()


def shards(
    hidden, code_ids, lengths, weight_in, weight_query, weight_key, weight_value, weight_out,
    norm_gain, tables, upstream,
):
    hbm = pl.BlockSpec(memory_space=pl.ANY)

    def scratch(dtype, *shape):
        return pltpu.VMEM(shape, dtype)

    block = (LV, FR, COLS)
    shapes = (
        jax.ShapeDtypeStruct((OWN, LV, WIDTH), BF16),
        jax.ShapeDtypeStruct((FR, WIDTH), BF16),
        jax.ShapeDtypeStruct((ENT, LV, COLS), F32),
    )
    results = pl.pallas_call(
        kernel,
        out_shape=shapes,
        in_specs=[hbm] * 11,
        out_specs=(hbm, hbm, hbm),
        scratch_shapes=[
            scratch(BF16, OWN, LV, WIDTH),
            scratch(BF16, FR, WIDTH),
            scratch(F32, ENT, LV, COLS),
            scratch(BF16, ENT, LV, COLS),
            scratch(BF16, OWN, LV, WIDTH),
            scratch(jnp.int32, 8, FR),
            pltpu.SMEM((4,), jnp.int32),
            scratch(F32, 1, WIDTH),
            scratch(BF16, FR, WIDTH),
            scratch(BF16, WIDTH, WIDTH),
            scratch(BF16, WIDTH, COLS),
            scratch(BF16, WIDTH, COLS),
            scratch(BF16, WIDTH, COLS),
            scratch(BF16, COLS, WIDTH),
            scratch(jnp.int32, 8, FR),
            scratch(jnp.int32, NY, 8, FR),
            scratch(BF16, LV, RANGE, COLS),
            scratch(BF16, LV, NY * FR, RANGE),
            scratch(BF16, LV, RANGE, NY * FR),
            scratch(BF16, LV, FR, WIDTH),
            scratch(BF16, 4, FR, COLS),
            scratch(BF16, 2, FR, COLS),
            scratch(BF16, FR, COLS),
            scratch(BF16, FR, COLS),
            scratch(BF16, NY, *block),
            scratch(BF16, 2, LV, FR // 2, COLS),
            scratch(BF16, 2, *block),
            scratch(F32, *block),
            scratch(BF16, 4, *block),
            scratch(BF16, LV, FR, WIDTH),
            scratch(F32, LV, FR, 128),
            scratch(BF16, *block),
            scratch(BF16, *block),
            scratch(BF16, *block),
            scratch(BF16, *block),
            scratch(BF16, 14, FR, COLS),
            scratch(F32, 14, FR, COLS),
            scratch(BF16, *block),
            scratch(BF16, *block),
            scratch(BF16, *block),
            scratch(BF16, *block),
            scratch(F32, *block),
            scratch(F32, *block),
            scratch(BF16, 3, *block),
            scratch(F32, *block),
            scratch(BF16, 2, *block),
            scratch(BF16, *block),
            scratch(BF16, *block),
            scratch(F32, LV, FR, 128),
            scratch(F32, 4, 8, FR),
            scratch(F32, LV, FR, 128),
            scratch(BF16, LV, FR, WIDTH),
            scratch(BF16, 2, LV, OWN, WIDTH),
            scratch(BF16, LV, OWN, WIDTH),
            scratch(BF16, LV, OWN, WIDTH),
            scratch(BF16, LV, NY * FR, COLS),
            scratch(BF16, 4, FR, COLS),
            scratch(F32, LV, RANGE, COLS),
            scratch(BF16, 2, LV, 2, ENT, COLS),
            scratch(BF16, 2, LV, 2, ENT, COLS),
            scratch(BF16, 2, LV, 2, ENT // 2, COLS),
            scratch(BF16, 2, LV, 2, ENT // 2, COLS),
            scratch(BF16, LV, 3, ENT, COLS),
            scratch(BF16, LV, 3, ENT, COLS),
            scratch(BF16, LV, 2, ENT, COLS),
            scratch(BF16, LV, 2, ENT, COLS),
            scratch(BF16, 4, LV, ENT, COLS),
            scratch(BF16, 4, LV, ENT, COLS),
            pltpu.SemaphoreType.DMA((14,)),
            pltpu.SemaphoreType.DMA((COPIES,)),
            pltpu.SemaphoreType.DMA((COPIES,)),
        ],
        compiler_params=pltpu.CompilerParams(
            collective_id=0, has_side_effects=True, vmem_limit_bytes=VMEM_BYTES
        ),
        name="layer",
    )(
        code_ids.T,
        lengths,
        norm_gain.reshape(1, WIDTH),
        tables,
        upstream,
        hidden,
        weight_in,
        weight_query,
        weight_key,
        weight_value,
        weight_out,
    )
    return pl.pallas_call(
        hand_over,
        out_shape=shapes,
        in_specs=[hbm] * 3,
        out_specs=(hbm, hbm, hbm),
        scratch_shapes=[pltpu.VMEM(x.shape, x.dtype) for x in shapes] + [pltpu.SemaphoreType.DMA((6,))],
        compiler_params=pltpu.CompilerParams(vmem_limit_bytes=VMEM_BYTES),
        name="hand_over",
    )(*results)


def solution(mesh):
    placed = (
        P("seq", "lvl"),
        P("seq", None),
        P(),
        P("lvl", None),
        P(None, "lvl"),
        P(None, "lvl"),
        P(None, "lvl"),
        P("lvl", None),
        P(),
        P("seq", None, "lvl"),
        P(("seq", "lvl"), None, None),
    )
    return jax.shard_map(
        shards,
        mesh=mesh,
        in_specs=placed,
        out_specs=(P(("seq", "lvl"), None, None), P("seq", "lvl"), P("seq", None, "lvl")),
        check_vma=False,
    )
```

```python
import math

import jax
import jax.numpy as jnp
from jax import lax
from jax.experimental import pallas as pl
from jax.experimental.pallas import tpu as pltpu
from jax.sharding import PartitionSpec as P

HEADS = 16
EPSILON = 1e-05
MESH = pl.DeviceIdType.MESH
F32 = jnp.float32
BF16 = jnp.bfloat16

NY, NZ = 4, 8
LV = 4
FR = 128
OWN = 32
COLS = 256
WIDTH = 1024
ENT = 32
RANGE = 512
COPIES = 192
VMEM_BYTES = 56 << 20


def dot(a, b):
    return lax.dot_general(a, b, (((1,), (0,)), ((), ())), preferred_element_type=F32)


def dot_nt(a, b):
    return lax.dot_general(a, b, (((1,), (1,)), ((), ())), preferred_element_type=F32)


def kernel(
    codes_hbm, lens_hbm, gain_hbm, tab_hbm, up_hbm, hid_hbm, win_hbm, wq_hbm, wk_hbm, wv_hbm, wo_hbm,
    out_hbm, hg_hbm, tg_hbm,
    out_ref, hg_ref, tg_ref,
    tab_in, up_in, codes_ref, lens_ref, gain_ref, hid_ref, win, wq, wk, wv, wo,
    nbr, raw, prev, tab, oh, oht, ups, ctx_send, ctx_core, ctx_mid, ctx_x,
    look, relay, fin, stream_own, streams, normed, scale,
    qs, ks, vs, gms, prod, sums, mix, gqs, gks, gvs, gk_sum, gv_sum,
    pn, pn_own, pn_core, pn_mid, pn_x, stat_wide, stat, stat_col,
    opart, o_core, o_mid, o_x,
    eg, cgs, grads, f3_send, f3_recv, f4_send, f4_recv, c1_send, c1_recv, c2_send, c2_recv, d_send, d_recv,
    local_sem, ssem, rsem,
):
    seq = lax.axis_index("seq")
    lvl = lax.axis_index("lvl")
    y = lax.div(seq, 16)
    xl = lax.rem(lax.div(seq, 8), 2)
    z = lax.rem(seq, 8)
    xh = lax.div(lvl, 2)
    core = lax.rem(lvl, 2)

    def device(dy=0, dx=0, dz=0, dh=0, dc=0):
        yy = lax.rem(y + dy + NY, NY)
        xx = 1 - xl if dx else xl
        zz = lax.rem(z + dz + NZ, NZ)
        hh = 1 - xh if dh else xh
        cc = 1 - core if dc else core
        return (yy * 16 + xx * 8 + zz, hh * 2 + cc)

    shifts = (0, 16, 48, 32)
    seq_next = [(lax.rem(seq + 1 + shift, 64), lvl) for shift in shifts]
    seq_back = [(lax.rem(seq + 127 - shift, 64), lvl) for shift in shifts]
    y_up, y_down, y_far = device(dy=1), device(dy=-1), device(dy=2)
    z_up, z_down, z_up2, z_down2 = device(dz=1), device(dz=-1), device(dz=2), device(dz=-2)
    x_near, x_far, mate, cross = device(dx=1), device(dh=1), device(dc=1), device(dh=1, dc=1)
    lvl_far = (1 - xh) * 2 + core
    lvl_mate = xh * 2 + 1 - core
    lvl_cross = (1 - xh) * 2 + 1 - core

    started = []

    def send(src, dst, target):
        i = len(started)
        copy = pltpu.make_async_remote_copy(
            src_ref=src, dst_ref=dst, send_sem=ssem.at[i], recv_sem=rsem.at[i],
            device_id=target, device_id_type=MESH,
        )
        copy.start()
        started.append(copy)
        return copy

    def push(ref, target):
        return send(ref, ref, target)

    def rows(start, size):
        return pl.ds(pl.multiple_of(start, size), size)

    def block_rows(xx, zz):
        return rows((xx * 8 + lax.rem(zz + NZ, NZ)) * ENT, ENT)

    own_rows = block_rows(xl, z)
    own_frames = rows(lvl * OWN, OWN)
    far_frames = rows(lvl_far * OWN, OWN)
    mate_frames = rows(lvl_mate * OWN, OWN)
    cross_frames = rows(lvl_cross * OWN, OWN)

    codes_ref[...] = jnp.zeros((8, FR), jnp.int32)
    fetch = {}
    for i, (name, a, b) in enumerate(
        (
            ("tab", tab_hbm, tab_in),
            ("codes", codes_hbm, codes_ref.at[0:LV]),
            ("hid", hid_hbm, hid_ref),
            ("win", win_hbm, win),
            ("ups", up_hbm, up_in),
            ("lens", lens_hbm, lens_ref),
            ("gain", gain_hbm, gain_ref),
            ("wo", wo_hbm, wo),
            ("wq", wq_hbm, wq),
            ("wk", wk_hbm, wk),
            ("wv", wv_hbm, wv),
        )
    ):
        fetch[name] = pltpu.make_async_copy(a, b, local_sem.at[i])
        fetch[name].start()

    barrier = pltpu.get_barrier_semaphore()
    for source in (z_up, z_down, z_up2, z_down2, x_near, y_up, y_down, y_far, mate, x_far, cross, *seq_back):
        pl.semaphore_signal(barrier, inc=1, device_id=source, device_id_type=MESH)
    fetch["hid"].wait()
    fetch["win"].wait()
    part = dot(hid_ref[...], win[...])
    for b in range(4):
        ctx_send[b] = part[:, b * COLS : (b + 1) * COLS].astype(BF16)
    fetch["tab"].wait()
    for k in range(LV):
        tab[k, own_rows, :] = tab_in[:, k, :]
    fetch["codes"].wait()
    pl.semaphore_wait(barrier, 15)

    def block(half, xx, zz):
        return tab.at[2 * half : 2 * half + 2, block_rows(xx, zz)]

    own = [block(h, xl, z) for h in range(2)]
    up2, down2, up1, down1, near_own = [], [], [], [], []
    for h in range(2):
        up2.append(push(own[h], z_up2))
        down2.append(push(own[h], z_down2))
        near_own.append(push(own[h], x_near))
        up1.append(push(own[h], z_up))
        down1.append(push(own[h], z_down))
    code_copies = [send(codes_ref, nbr.at[i], target) for i, target in enumerate(seq_next)]
    code_copies += [
        send(codes_ref, raw.at[1], y_up),
        send(codes_ref, raw.at[2], y_down),
        send(codes_ref, raw.at[3], y_far),
    ]
    ctx_copies = [
        send(ctx_send.at[lvl_cross], ctx_core.at[0], mate),
        send(ctx_send.at[lvl_mate], ctx_core.at[1], mate),
    ]
    fetch["ups"].wait()
    for k in range(LV):
        ups[k, own_frames, :] = up_in[:, k, :]
    up_mate = [push(ups.at[k, own_frames], mate) for k in range(LV)]

    near2, up3, down3, near1 = [], [], [], []
    for h in range(2):
        up2[h].wait_recv()
        near2.append(push(block(h, xl, z - 2), x_near))
        up3.append(push(block(h, xl, z - 2), z_up))
        if h == 0:
            end_up = push(block(0, xl, z - 2), z_up2)
        down2[h].wait_recv()
        near2.append(push(block(h, xl, z + 2), x_near))
        down3.append(push(block(h, xl, z + 2), z_down))
        if h == 1:
            end_down = push(block(1, xl, z + 2), z_down2)
    for h in range(2):
        up1[h].wait_recv()
        near1.append(push(block(h, xl, z - 1), x_near))
        down1[h].wait_recv()
        near1.append(push(block(h, xl, z + 1), x_near))
    ctx_copies[0].wait_recv()
    ctx_mid[...] = (ctx_send[lvl_far].astype(F32) + ctx_core[0].astype(F32)).astype(BF16)
    ctx_far = send(ctx_mid, ctx_x, x_far)

    for copy in code_copies:
        copy.wait_recv()
    raw[0] = codes_ref[...]
    lane8 = lax.broadcasted_iota(jnp.int32, (8, FR), 1)
    sub8 = lax.broadcasted_iota(jnp.int32, (8, FR), 0)
    for slot, shift in enumerate(shifts):
        codes = raw[slot]
        shifted = pltpu.roll(codes, 1, 1)
        incoming = pltpu.roll(nbr[slot], 1, 1)
        holder = lax.rem(seq + 64 - shift, 64)
        incoming = jnp.where(jnp.broadcast_to(holder, (8, FR)) == 0, 0, incoming)
        shifted = jnp.where(lane8 == 0, incoming, shifted)
        first_row = jnp.broadcast_to(shifted[LV - 1 : LV, :], (8, FR))
        prev[slot] = jnp.where(sub8 == 0, first_row, pltpu.roll(codes, 1, 0))

    first = y * RANGE
    by_lane = lax.broadcasted_iota(jnp.int32, (FR, RANGE), 1) + first
    by_row = lax.broadcasted_iota(jnp.int32, (RANGE, FR), 0) + first
    for slot in range(NY):
        codes = prev[slot]
        turned = jnp.transpose(
            jnp.concatenate([codes.astype(F32), jnp.zeros((FR - 8, FR), F32)], axis=0)
        ).astype(jnp.int32)
        for k in range(LV):
            column = jnp.broadcast_to(turned[:, k : k + 1], (FR, RANGE))
            oh[k, slot * FR : (slot + 1) * FR, :] = jnp.where(column == by_lane, 1.0, 0.0).astype(BF16)

    far_up, far_down = [], []
    for h in range(2):
        near2[2 * h].wait_recv()
        far_up.append(push(block(h, 1 - xl, z - 2), z_up))
        if h == 0:
            far_end_up = push(block(0, 1 - xl, z - 2), z_up2)
        near2[2 * h + 1].wait_recv()
        far_down.append(push(block(h, 1 - xl, z + 2), z_down))
        if h == 1:
            far_end_down = push(block(1, 1 - xl, z + 2), z_down2)
    up_far = [push(ups.at[k, own_frames], x_far) for k in range(LV)]

    for slot in range(NY):
        codes = prev[slot]
        for k in range(LV):
            row = jnp.broadcast_to(codes[k : k + 1, :], (RANGE, FR))
            oht[k, :, slot * FR : (slot + 1) * FR] = jnp.where(row == by_row, 1.0, 0.0).astype(BF16)
    fetch["lens"].wait()
    frame = lax.broadcasted_iota(jnp.int32, (FR, COLS), 0) + seq * FR
    begin = jnp.int32(0)
    retain = jnp.ones((FR, COLS), F32)
    for i in range(4):
        retain = jnp.where(frame == begin, 0.0, retain)
        begin = begin + lens_ref[i]

    top, low = slice(0, FR // 2), slice(FR // 2, FR)
    relay_up, relay_down = [], []
    fin_up = [[None, None] for _ in range(LV)]
    fin_down = [[None, None] for _ in range(LV)]

    def find(k):
        found = dot(oh[k], tab[k]).astype(BF16)
        for slot in (3, 2, 1, 0):
            look[slot, k] = found[slot * FR : (slot + 1) * FR, :]
        relay_up.append(send(look.at[3, k, top], relay.at[0, k], y_up))
        relay_down.append(send(look.at[3, k, low], relay.at[1, k], y_down))

    def direct(k):
        fin_up[k][1] = send(look.at[2, k, low], fin.at[0, k, low], y_up)
        fin_down[k][0] = send(look.at[1, k, top], fin.at[1, k, top], y_down)

    def relayed(k):
        relay_up[k].wait_recv()
        look[2, k, top] = look[2, k, top] + relay[0, k]
        fin_up[k][0] = send(look.at[2, k, top], fin.at[0, k, top], y_up)
        relay_down[k].wait_recv()
        look[1, k, low] = look[1, k, low] + relay[1, k]
        fin_down[k][1] = send(look.at[1, k, low], fin.at[1, k, low], y_down)

    far, near, passed = [], [], []

    def stream(k):
        for copy in fin_up[k] + fin_down[k]:
            copy.wait_recv()
        embedded = look[0, k].astype(F32) + fin[0, k].astype(F32) + fin[1, k].astype(F32)
        if k == 0:
            embedded = retain * embedded
        own = context + embedded
        stream_own[k] = own
        streams[lvl, k] = own.astype(BF16)
        far.append(push(streams.at[lvl, k], x_far))
        near.append(push(streams.at[lvl, k], mate))

    def pass_stream(k):
        far[k].wait_recv()
        passed.append(push(streams.at[lvl_far, k], mate))

    def blocks_in(h):
        for copy in (up3[h], down3[h], near_own[h], near1[2 * h], near1[2 * h + 1], far_up[h], far_down[h]):
            copy.wait_recv()

    blocks_in(0)
    end_up.wait_recv()
    far_end_up.wait_recv()
    find(0)
    find(1)
    direct(0)
    blocks_in(1)
    end_down.wait_recv()
    far_end_down.wait_recv()
    find(2)
    find(3)
    direct(1)
    relayed(0)
    relayed(1)
    direct(2)
    relayed(2)
    direct(3)
    relayed(3)
    ctx_copies[1].wait_recv()
    ctx_far.wait_recv()
    context = ctx_send[lvl].astype(F32) + ctx_core[1].astype(F32) + ctx_x[...].astype(F32)
    stream(0)
    stream(1)
    stream(2)
    stream(3)
    up_pass = []
    for k in range(LV):
        up_far[k].wait_recv()
        up_pass.append(push(ups.at[k, far_frames], mate))
    pass_stream(0)
    pass_stream(1)
    fetch["wo"].wait()
    for k in range(LV):
        up_mate[k].wait_recv()
        up_pass[k].wait_recv()
    gms[...] = dot_nt(ups[...].reshape(LV * FR, WIDTH), wo[...]).astype(BF16).reshape(LV, FR, COLS)
    for name in ("gain", "wq", "wk", "wv"):
        fetch[name].wait()

    head_row = lax.shift_right_logical(lax.broadcasted_iota(jnp.int32, (COLS, COLS), 0), 6)
    head_col = lax.shift_right_logical(lax.broadcasted_iota(jnp.int32, (COLS, COLS), 1), 6)
    same_head = jnp.where(head_row == head_col, 1.0, 0.0).astype(BF16)
    scaling = 1.0 / math.sqrt(WIDTH // HEADS)

    def norm(a):
        near[a].wait_recv()
        passed[a].wait_recv()

        def norm_body(i, carry):
            r = rows(i * 32, 32)
            blocks = [streams[b, a, r, :].astype(F32) for b in range(4)]
            total = blocks[0] * blocks[0]
            for b in range(1, 4):
                total = total + blocks[b] * blocks[b]
            scaler = lax.rsqrt(jnp.sum(total, axis=1, keepdims=True) * (1.0 / WIDTH) + EPSILON)
            scale[a, r, :] = jnp.broadcast_to(scaler, (32, 128))
            for b in range(4):
                normed[a, r, b * COLS : (b + 1) * COLS] = (
                    blocks[b] * scaler * gain_ref[:, b * COLS : (b + 1) * COLS]
                ).astype(BF16)
            return carry

        lax.fori_loop(0, 4, norm_body, 0)

    def attend_level(a, base):
        def attend_body(i, carry):
            r = rows(lax.div(i, 2) * 16, 16)
            c = rows(lax.rem(i, 2) * 128, 128)
            q = qs[a, r, c].astype(F32)
            g = gms[a, r, c].astype(F32)
            raised = [jnp.exp(sums[base + b, r, c] * scaling) for b in range(a + 1)]
            total = raised[0]
            for b in range(1, a + 1):
                total = total + raised[b]
            inverse = 1.0 / total
            weights = [x * inverse for x in raised]
            rounded = [x.astype(BF16).astype(F32) for x in weights]
            slopes = [sums[base + a + 1 + b, r, c] for b in range(a + 1)]
            mixed = rounded[0] * vs[0, r, c].astype(F32)
            mean = weights[0] * slopes[0]
            for b in range(1, a + 1):
                mixed = mixed + rounded[b] * vs[b, r, c].astype(F32)
                mean = mean + weights[b] * slopes[b]
            mix[a, r, c] = mixed.astype(BF16)
            grad_query = None
            for b in range(a + 1):
                grad_score = (weights[b] * (slopes[b] - mean) * scaling).astype(BF16).astype(F32)
                term_q = grad_score * ks[b, r, c].astype(F32)
                term_k = grad_score * q
                term_v = rounded[b] * g
                grad_query = term_q if b == 0 else grad_query + term_q
                if a > b:
                    term_k = term_k + gk_sum[b, r, c]
                    term_v = term_v + gv_sum[b, r, c]
                if a == LV - 1:
                    gks[b, r, c] = term_k.astype(BF16)
                    gvs[b, r, c] = term_v.astype(BF16)
                else:
                    gk_sum[b, r, c] = term_k
                    gv_sum[b, r, c] = term_v
            gqs[a, r, c] = grad_query.astype(BF16)
            return carry

        lax.fori_loop(0, 16, attend_body, 0)

    def two_levels(first):
        x = normed[first : first + 2].reshape(2 * FR, WIDTH)
        for w, target in ((wq, qs), (wk, ks), (wv, vs)):
            target[first : first + 2] = dot(x, w[...]).astype(BF16).reshape(2, FR, COLS)
        count = 2 * (first + 1) + 2 * (first + 2)

        def product_body(i, carry):
            r = rows(i * 16, 16)
            base = 0
            for a in (first, first + 1):
                q = qs[a, r, :].astype(F32)
                g = gms[a, r, :].astype(F32)
                for b in range(a + 1):
                    prod[base + b, r, :] = (q * ks[b, r, :].astype(F32)).astype(BF16)
                    prod[base + a + 1 + b, r, :] = (g * vs[b, r, :].astype(F32)).astype(BF16)
                base += 2 * (a + 1)
            return carry

        lax.fori_loop(0, 8, product_body, 0)
        sums[0:count] = dot(prod[0:count].reshape(count * FR, COLS), same_head).reshape(count, FR, COLS)
        attend_level(first, 0)
        attend_level(first + 1, 2 * (first + 1))

    norm(0)
    norm(1)
    pass_stream(2)
    two_levels(0)
    norm(2)
    pass_stream(3)
    norm(3)
    two_levels(2)

    gq = gqs[...].reshape(LV * FR, COLS)
    gk = gks[...].reshape(LV * FR, COLS)
    gv = gvs[...].reshape(LV * FR, COLS)

    def partial(owner):
        w = rows(owner * COLS, COLS)
        total = dot_nt(gq, wq[w, :]) + dot_nt(gk, wk[w, :]) + dot_nt(gv, wv[w, :])
        return total.reshape(LV, FR, COLS)

    pn[0] = partial(lvl_cross).astype(BF16)
    pn_cross = [send(pn.at[0, k], pn_core.at[0, k], mate) for k in range(LV)]
    def stat_body(i, carry):
        r = rows(i * 32, 32)
        for k in range(LV):
            share = (
                qs[k, r, :].astype(F32) * gqs[k, r, :].astype(F32)
                + ks[k, r, :].astype(F32) * gks[k, r, :].astype(F32)
                + vs[k, r, :].astype(F32) * gvs[k, r, :].astype(F32)
            )
            stat_wide[k, r, :] = jnp.broadcast_to(jnp.sum(share, axis=1, keepdims=True), (32, 128))
        return carry

    lax.fori_loop(0, 4, stat_body, 0)
    eye = lax.broadcasted_iota(jnp.int32, (FR, FR), 0) == lax.broadcasted_iota(jnp.int32, (FR, FR), 1)
    for k in range(LV):
        stat[0, k : k + 1, :] = jnp.sum(jnp.where(eye, stat_wide[k], 0.0), axis=0, keepdims=True)
    stat[0, LV:, :] = jnp.zeros((8 - LV, FR), F32)
    stat_copies = [
        send(stat.at[0], stat.at[1], x_far),
        send(stat.at[0], stat.at[2], mate),
        send(stat.at[0], stat.at[3], cross),
    ]

    pn[2] = partial(lvl_far).astype(BF16)
    pn_far = []
    for k in range(LV):
        pn_cross[k].wait_recv()
        pn_mid[k] = (pn[2, k].astype(F32) + pn_core[0, k].astype(F32)).astype(BF16)
        pn_far.append(send(pn_mid.at[k], pn_x.at[k], x_far))
    pn[1] = partial(lvl_mate).astype(BF16)
    pn_mate = [send(pn.at[1, k], pn_core.at[1, k], mate) for k in range(LV)]
    opart[...] = dot(mix[...].reshape(LV * FR, COLS), wo[...]).astype(BF16).reshape(LV, FR, WIDTH)
    o_copies = [
        send(opart.at[:, cross_frames], o_core.at[0], mate),
        send(opart.at[:, mate_frames], o_core.at[1], mate),
    ]
    pn_own[...] = partial(lvl)

    for copy in stat_copies:
        copy.wait_recv()
    stat_all = (stat[0] + stat[1] + stat[2] + stat[3]) * (1.0 / WIDTH)
    for k in range(LV):
        column = jnp.sum(
            jnp.where(eye, jnp.broadcast_to(stat_all[k : k + 1, :], (FR, FR)), 0.0), axis=1, keepdims=True
        )
        stat_col[k] = jnp.broadcast_to(column, (FR, 128))

    own_cols = rows(lvl * COLS, COLS)
    gain = gain_ref[:, own_cols]
    context_grads = []
    g_copies = []

    def stream_grad(k):
        pn_mate[k].wait_recv()
        pn_far[k].wait_recv()
        grad_normed = pn_own[k] + pn_core[1, k].astype(F32) + pn_x[k].astype(F32)
        scaler = scale[k][:, 0:1]
        unit = stream_own[k] * scaler
        grad = ups[k, :, own_cols].astype(F32) + scaler * (gain * grad_normed - unit * stat_col[k][:, 0:1])
        context_grads.append(grad)
        eg[k, 0:FR, :] = (retain * grad if k == 0 else grad).astype(BF16)
        copies = []
        if k == LV - 1:
            copies.append(send(eg.at[k, 0:FR], eg.at[k, 3 * FR : 4 * FR], y_far))
        copies.append(send(eg.at[k, 0:FR], eg.at[k, FR : 2 * FR], y_up))
        copies.append(send(eg.at[k, 0:FR], eg.at[k, 2 * FR : 3 * FR], y_down))
        g_copies.append(copies)

    def pass_grad(k):
        copy_up, copy_down = g_copies[k]
        copy_up.wait_recv()
        pass_up = send(eg.at[k, FR : FR + FR // 2], eg.at[k, 3 * FR : 3 * FR + FR // 2], y_up)
        copy_down.wait_recv()
        pass_down = send(
            eg.at[k, 2 * FR + FR // 2 : 3 * FR], eg.at[k, 3 * FR + FR // 2 : 4 * FR], y_down
        )
        g_copies[k] = [pass_up, pass_down]

    stream_grad(0)
    stream_grad(1)
    o_copies[0].wait_recv()
    o_mid[...] = (opart[:, far_frames, :].astype(F32) + o_core[0].astype(F32)).astype(BF16)
    stream_grad(2)
    o_far = send(o_mid, o_x, x_far)
    pass_grad(0)
    stream_grad(3)
    pass_grad(1)
    cgs[lvl] = (context_grads[0] + context_grads[1] + context_grads[2] + context_grads[3]).astype(BF16)
    cg_far = push(cgs.at[lvl], x_far)
    cg_mate = push(cgs.at[lvl], mate)
    pass_grad(2)

    half = ENT // 2
    fringe, crossed, direct_sums = {}, {}, {}

    def packed(xx, zz, k):
        return grads[k, block_rows(xx, zz), :]

    def fringe_step(k):
        for copy in g_copies[k]:
            copy.wait_recv()
        grads[k] = dot(oht[k], eg[k])
        for j, xx in enumerate((xl, 1 - xl)):
            f3_send[0, k, j] = packed(xx, z - 3, k).astype(BF16)
            f3_send[1, k, j] = packed(xx, z + 3, k).astype(BF16)
            value = packed(xx, z + 4, k).astype(BF16)
            f4_send[0, k, j] = value[0:half, :]
            f4_send[1, k, j] = value[half:, :]
        fringe[k] = (
            [
                send(f3_send.at[0, k], f3_recv.at[0, k], z_down),
                send(f3_send.at[1, k], f3_recv.at[1, k], z_up),
                send(f4_send.at[0, k], f4_recv.at[0, k], z_down2),
                send(f4_send.at[1, k], f4_recv.at[1, k], z_up2),
            ]
        )
        for o in range(3):
            c1_send[k, o] = packed(1 - xl, z + o - 1, k).astype(BF16)
        crossed[k] = [send(c1_send.at[k], c1_recv.at[k], x_near)]

    def two_away(side, j, k):
        value = packed(xl if j == 0 else 1 - xl, z - 2 if side == 0 else z + 2, k)
        value = value + f3_recv[side, k, j].astype(F32)
        ends = f4_recv[side, k, j].astype(F32)
        zeros = jnp.zeros((half, COLS), F32)
        return value + jnp.concatenate([ends, zeros] if side == 0 else [zeros, ends], axis=0)

    def cross_step(k):
        for copy in fringe[k]:
            copy.wait_recv()
        for side in range(2):
            c2_send[k, side] = two_away(side, 1, k).astype(BF16)
        crossed[k].append(send(c2_send.at[k], c2_recv.at[k], x_near))

    def direct_step(k):
        for copy in crossed[k]:
            copy.wait_recv()
        for side in range(2):
            value = two_away(side, 0, k) + c2_recv[k, side].astype(F32)
            d_send[2 + side, k] = value.astype(BF16)
            value = packed(xl, z + 2 * side - 1, k) + c1_recv[k, 2 * side].astype(F32)
            d_send[side, k] = value.astype(BF16)
        direct_sums[k] = (
            [
                send(d_send.at[i, k], d_recv.at[i, k], target)
                for i, target in ((2, z_down2), (3, z_up2), (0, z_down), (1, z_up))
            ]
        )

    def final_step(k):
        value = packed(xl, z, k) + c1_recv[k, 1].astype(F32)
        for copy in direct_sums[k]:
            copy.wait_recv()
        for i in range(4):
            value = value + d_recv[i, k].astype(F32)
        tg_ref[:, k, :] = value

    fringe_step(0)
    fringe_step(1)
    fringe_step(3)
    fringe_step(2)
    cross_step(0)
    cross_step(1)
    direct_step(0)
    cross_step(3)
    cross_step(2)
    cg_far.wait_recv()
    cg_pass = push(cgs.at[lvl_far], mate)
    direct_step(1)
    direct_step(3)
    direct_step(2)

    cg_mate.wait_recv()
    cg_pass.wait_recv()
    whole = jnp.concatenate([cgs[b] for b in range(4)], axis=1)
    hg_ref[...] = dot_nt(whole, win[...]).astype(BF16)
    hg_copy = pltpu.make_async_copy(hg_ref, hg_hbm, local_sem.at[11])
    hg_copy.start()

    o_copies[1].wait_recv()
    o_far.wait_recv()
    for k in range(LV):
        base = jnp.concatenate([streams[b, k, own_frames, :] for b in range(4)], axis=1).astype(F32)
        out_ref[:, k, :] = (
            base + opart[k, own_frames, :].astype(F32) + o_core[1, k].astype(F32) + o_x[k].astype(F32)
        ).astype(BF16)
    out_copy = pltpu.make_async_copy(out_ref, out_hbm, local_sem.at[12])
    out_copy.start()
    for k in range(LV):
        final_step(k)
    tg_copy = pltpu.make_async_copy(tg_ref, tg_hbm, local_sem.at[13])
    tg_copy.start()

    for copy in started:
        copy.wait_send()
    for copy in (hg_copy, out_copy, tg_copy):
        copy.wait()
    assert len(started) <= COPIES


def hand_over(out_in, hg_in, tg_in, out_ref, hg_ref, tg_ref, out_held, hg_held, tg_held, sem):
    held = (out_held, hg_held, tg_held)
    first = [
        pltpu.make_async_copy(a, b, sem.at[i]) for i, (a, b) in enumerate(zip((out_in, hg_in, tg_in), held))
    ]
    second = [
        pltpu.make_async_copy(a, b, sem.at[3 + i])
        for i, (a, b) in enumerate(zip(held, (out_ref, hg_ref, tg_ref)))
    ]
    for copy in first:
        copy.start()
    for before, after in zip(first, second):
        before.wait()
        after.start()
    for copy in second:
        copy.wait()


def shards(
    hidden, code_ids, lengths, weight_in, weight_query, weight_key, weight_value, weight_out,
    norm_gain, tables, upstream,
):
    hbm = pl.BlockSpec(memory_space=pl.ANY)

    def scratch(dtype, *shape):
        return pltpu.VMEM(shape, dtype)

    block = (LV, FR, COLS)
    shapes = (
        jax.ShapeDtypeStruct((OWN, LV, WIDTH), BF16),
        jax.ShapeDtypeStruct((FR, WIDTH), BF16),
        jax.ShapeDtypeStruct((ENT, LV, COLS), F32),
    )
    results = pl.pallas_call(
        kernel,
        out_shape=shapes,
        in_specs=[hbm] * 11,
        out_specs=(hbm, hbm, hbm),
        scratch_shapes=[
            scratch(BF16, OWN, LV, WIDTH),
            scratch(BF16, FR, WIDTH),
            scratch(F32, ENT, LV, COLS),
            scratch(BF16, ENT, LV, COLS),
            scratch(BF16, OWN, LV, WIDTH),
            scratch(jnp.int32, 8, FR),
            pltpu.SMEM((4,), jnp.int32),
            scratch(F32, 1, WIDTH),
            scratch(BF16, FR, WIDTH),
            scratch(BF16, WIDTH, WIDTH),
            scratch(BF16, WIDTH, COLS),
            scratch(BF16, WIDTH, COLS),
            scratch(BF16, WIDTH, COLS),
            scratch(BF16, COLS, WIDTH),
            scratch(jnp.int32, NY, 8, FR),
            scratch(jnp.int32, NY, 8, FR),
            scratch(jnp.int32, NY, 8, FR),
            scratch(BF16, LV, RANGE, COLS),
            scratch(BF16, LV, NY * FR, RANGE),
            scratch(BF16, LV, RANGE, NY * FR),
            scratch(BF16, LV, FR, WIDTH),
            scratch(BF16, 4, FR, COLS),
            scratch(BF16, 2, FR, COLS),
            scratch(BF16, FR, COLS),
            scratch(BF16, FR, COLS),
            scratch(BF16, NY, *block),
            scratch(BF16, 2, LV, FR // 2, COLS),
            scratch(BF16, 2, *block),
            scratch(F32, *block),
            scratch(BF16, 4, *block),
            scratch(BF16, LV, FR, WIDTH),
            scratch(F32, LV, FR, 128),
            scratch(BF16, *block),
            scratch(BF16, *block),
            scratch(BF16, *block),
            scratch(BF16, *block),
            scratch(BF16, 14, FR, COLS),
            scratch(F32, 14, FR, COLS),
            scratch(BF16, *block),
            scratch(BF16, *block),
            scratch(BF16, *block),
            scratch(BF16, *block),
            scratch(F32, *block),
            scratch(F32, *block),
            scratch(BF16, 3, *block),
            scratch(F32, *block),
            scratch(BF16, 2, *block),
            scratch(BF16, *block),
            scratch(BF16, *block),
            scratch(F32, LV, FR, 128),
            scratch(F32, 4, 8, FR),
            scratch(F32, LV, FR, 128),
            scratch(BF16, LV, FR, WIDTH),
            scratch(BF16, 2, LV, OWN, WIDTH),
            scratch(BF16, LV, OWN, WIDTH),
            scratch(BF16, LV, OWN, WIDTH),
            scratch(BF16, LV, NY * FR, COLS),
            scratch(BF16, 4, FR, COLS),
            scratch(F32, LV, RANGE, COLS),
            scratch(BF16, 2, LV, 2, ENT, COLS),
            scratch(BF16, 2, LV, 2, ENT, COLS),
            scratch(BF16, 2, LV, 2, ENT // 2, COLS),
            scratch(BF16, 2, LV, 2, ENT // 2, COLS),
            scratch(BF16, LV, 3, ENT, COLS),
            scratch(BF16, LV, 3, ENT, COLS),
            scratch(BF16, LV, 2, ENT, COLS),
            scratch(BF16, LV, 2, ENT, COLS),
            scratch(BF16, 4, LV, ENT, COLS),
            scratch(BF16, 4, LV, ENT, COLS),
            pltpu.SemaphoreType.DMA((14,)),
            pltpu.SemaphoreType.DMA((COPIES,)),
            pltpu.SemaphoreType.DMA((COPIES,)),
        ],
        compiler_params=pltpu.CompilerParams(
            collective_id=0, has_side_effects=True, vmem_limit_bytes=VMEM_BYTES
        ),
        name="layer",
    )(
        code_ids.T,
        lengths,
        norm_gain.reshape(1, WIDTH),
        tables,
        upstream,
        hidden,
        weight_in,
        weight_query,
        weight_key,
        weight_value,
        weight_out,
    )
    return pl.pallas_call(
        hand_over,
        out_shape=shapes,
        in_specs=[hbm] * 3,
        out_specs=(hbm, hbm, hbm),
        scratch_shapes=[pltpu.VMEM(x.shape, x.dtype) for x in shapes] + [pltpu.SemaphoreType.DMA((6,))],
        compiler_params=pltpu.CompilerParams(vmem_limit_bytes=VMEM_BYTES),
        name="hand_over",
    )(*results)


def solution(mesh):
    placed = (
        P("seq", "lvl"),
        P("seq", None),
        P(),
        P("lvl", None),
        P(None, "lvl"),
        P(None, "lvl"),
        P(None, "lvl"),
        P("lvl", None),
        P(),
        P("seq", None, "lvl"),
        P(("seq", "lvl"), None, None),
    )
    return jax.shard_map(
        shards,
        mesh=mesh,
        in_specs=placed,
        out_specs=(P(("seq", "lvl"), None, None), P("seq", "lvl"), P("seq", None, "lvl")),
        check_vma=False,
    )
```
